32 devices in a mesh: vocab: 8 (over y, x, core), seq: 4 (over z).
Axes of the slice: x: 2, y: 2, z: 4, core: 2. Of those that a mesh axis runs over, the one named last changes fastest.
Arguments:
- hidden_states: bfloat16 [256, 2560], P('seq'), may hold values from -16 to 16
- head_weight: bfloat16 [2560, 75968], P('seq', 'vocab'), may hold values from -3 to 3
- teacher_logits: bfloat16 [4, 64, 75968], P('seq', 'vocab'), may hold values from -20 to 330
Outputs:
- mean_divergence: float32 [], replicated
- hidden_grad: float32 [256, 2560], P('seq', 'vocab')
- head_grad: float32 [2560, 75968], P('seq', 'vocab')
The draws below stay inside these ranges and needn't reach their ends.
All inputs are finite; a program needn't handle non-finite values.
Results may differ from the reference program's by a relative error of at most 0.003.
Values may be sent and summed in bfloat16 or wider, within the bound.
No kernel may reach another device: no remote copies, remote signals or barrier semaphores. Data moves between devices by JAX's collectives and lax.ppermute only.
A program may use at most 256 MiB of HBM per device.

```python
import jax
import jax.numpy as jnp

D = 2560
VOCAB = 75968
TOK_DEV = 64
SEQ_SHARDS = 4
TOKENS = 256


anchor_count = 8


def shuffle_pattern(subkey):
    pattern = jnp.where(jnp.arange(D) < D // 2, 1.0, -1.0)
    return jax.random.permutation(subkey, pattern)


def anchors(key):
    key = jax.random.fold_in(key, 101)
    sign_key, flip_key, column_key = jax.random.split(key, 3)
    signs = 2.0 * jax.random.randint(sign_key, (anchor_count, D), 0, 2).astype(jnp.float32) - 1.0
    flips = jax.vmap(shuffle_pattern)(jax.random.split(flip_key, anchor_count))
    first_vec = signs / jnp.sqrt(float(D))
    second_vec = first_vec * flips
    columns = jax.random.permutation(column_key, VOCAB)[:2 * anchor_count]
    return (first_vec, second_vec, columns[:anchor_count], columns[anchor_count:])


def draw_head_weight(key, part):
    first_vec, second_vec, first_cols, second_cols = anchors(key)
    key = jax.random.fold_in(key, 7)
    values = 3.0 * jnp.clip(jax.random.normal(key, (D, VOCAB)), -6.0, 6.0) / jnp.sqrt(float(D))
    values = values.at[:, first_cols].set(first_vec.T)
    values = values.at[:, second_cols].set(second_vec.T)
    return values.astype(jnp.bfloat16)


def draw_hidden_states(key, part):
    key = jax.random.fold_in(key, 11)
    base_key = jax.random.fold_in(key, 0)
    values = jnp.clip(jax.random.normal(base_key, (TOKENS, D)), -6.0, 6.0)
    return values.astype(jnp.bfloat16)


def draw_teacher_logits(key, part):
    key = jax.random.fold_in(key, 13)
    base_key = jax.random.fold_in(key, 0)
    values = 3.0 * jnp.clip(jax.random.normal(base_key, (TOKENS, VOCAB)), -6.0, 6.0)
    return values.reshape(SEQ_SHARDS, TOK_DEV, VOCAB).astype(jnp.bfloat16)


def setup_inputs(seed: int = 0) -> dict:
    key_of = jax.random.split(jax.random.key(seed), 4)
    hidden_states = draw_hidden_states(jax.random.fold_in(key_of[3], 71), 0)
    head_weight = draw_head_weight(jax.random.fold_in(key_of[3], 71), 0)
    teacher_logits = draw_teacher_logits(jax.random.fold_in(key_of[3], 71), 0)
    return {"hidden_states": hidden_states, "head_weight": head_weight, "teacher_logits": teacher_logits}


LOSS_SCALE = 256.0


def reference(hidden_states, head_weight, teacher_logits):
    student = jnp.dot(hidden_states, head_weight, preferred_element_type=jnp.float32)
    teacher = teacher_logits.reshape(TOKENS, VOCAB).astype(jnp.float32)
    student_max = jnp.max(student, axis=1, keepdims=True)
    teacher_max = jnp.max(teacher, axis=1, keepdims=True)
    student_exp = jnp.exp(student - student_max)
    teacher_exp = jnp.exp(teacher - teacher_max)
    student_sum = jnp.sum(student_exp, axis=1, keepdims=True)
    teacher_sum = jnp.sum(teacher_exp, axis=1, keepdims=True)
    cross = jnp.sum(teacher_exp * (teacher - student), axis=1, keepdims=True)
    divergence = cross / teacher_sum - teacher_max - jnp.log(teacher_sum) + student_max + jnp.log(student_sum)
    mean_divergence = jnp.sum(divergence) / TOKENS
    grad = (LOSS_SCALE * (student_exp / student_sum - teacher_exp / teacher_sum)).astype(jnp.bfloat16)
    hidden_grad = jnp.dot(grad, head_weight.T, preferred_element_type=jnp.float32)
    head_grad = jnp.dot(hidden_states.T, grad, preferred_element_type=jnp.float32)
    return mean_divergence, hidden_grad, head_grad
```

```python
import jax
import jax.numpy as jnp
from jax import lax
from jax.sharding import PartitionSpec as P

LOSS_SCALE = 256.0


def body(hidden_states, head_weight, teacher_logits):
    seq_count = lax.axis_size("seq")
    vocab_count = lax.axis_size("vocab")
    half = seq_count // 2
    last = seq_count - 1
    z = lax.axis_index("seq")
    own_tokens, width = hidden_states.shape
    rows, cols = head_weight.shape
    per_dev = teacher_logits.shape[1]
    chunk = half * per_dev
    chunks = vocab_count
    total_tokens = own_tokens * seq_count

    mine = teacher_logits[0]
    held = [mine] + [
        lax.ppermute(mine, "seq", [(j, 0), (last - j, last)]) for j in range(1, half)
    ]
    held = jnp.concatenate(held, axis=0)
    pieces = jnp.stack([held[:, v * cols:(v + 1) * cols] for v in range(vocab_count)])
    teacher = lax.all_to_all(pieces, "vocab", split_axis=0, concat_axis=0, tiled=True)

    local_cols = lax.all_to_all(hidden_states, "seq", split_axis=1, concat_axis=0, tiled=True)
    by_block = local_cols.reshape(seq_count, vocab_count, per_dev, rows)
    ordered = jnp.stack([by_block[:half], by_block[half:][::-1]])
    ordered = ordered.transpose(0, 2, 1, 3, 4).reshape(total_tokens, rows)
    partial = jnp.dot(ordered, head_weight, preferred_element_type=jnp.float32)
    partial = partial.reshape(2, chunks, chunk, cols)

    def part(side, index):
        index = jnp.clip(index, 0, chunks - 1)
        return lax.dynamic_slice(partial, (side, index, 0, 0), (1, 1, chunk, cols))[0, 0]

    steps = chunks + seq_count - 2
    own_side = (z >= half).astype(jnp.int32)
    down = up = None
    students = []
    for s in range(steps):
        send_down = part(0, s - (last - z))
        send_up = part(1, s - z)
        if down is not None:
            send_down = send_down + down
            send_up = send_up + up
        down = lax.ppermute(
            send_down, "seq",
            [(d, d - 1) for d in range(1, seq_count) if 0 <= s - (last - d) < chunks])
        up = lax.ppermute(
            send_up, "seq", [(d, d + 1) for d in range(last) if 0 <= s - d < chunks])
        index = s - (seq_count - 2)
        if index >= 0:
            students.append(part(own_side, index) + jnp.where(z < half, down, up))

    divergence = jnp.zeros((), jnp.float32)
    grads = []
    for i in range(chunks):
        student = students[i]
        target = teacher[i].astype(jnp.float32)
        student_top = jnp.max(student, axis=1)
        target_top = jnp.max(target, axis=1)
        target_exp = jnp.exp(target - target_top[:, None])
        stats = jnp.stack([
            student_top,
            target_top,
            jnp.sum(jnp.exp(student - student_top[:, None]), axis=1),
            jnp.sum(target_exp, axis=1),
            jnp.sum(target_exp * (target - student), axis=1),
        ])
        stats = lax.all_gather(stats, "vocab", axis=0)
        student_max = jnp.max(stats[:, 0], axis=0)
        teacher_max = jnp.max(stats[:, 1], axis=0)
        student_scale = jnp.exp(stats[:, 0] - student_max)
        teacher_scale = jnp.exp(stats[:, 1] - teacher_max)
        student_sum = jnp.sum(stats[:, 2] * student_scale, axis=0)
        teacher_sum = jnp.sum(stats[:, 3] * teacher_scale, axis=0)
        cross = jnp.sum(stats[:, 4] * teacher_scale, axis=0)
        divergence = divergence + jnp.sum(
            cross / teacher_sum
            - teacher_max
            - jnp.log(teacher_sum)
            + student_max
            + jnp.log(student_sum)
        )
        grads.append((
            LOSS_SCALE * (
                jnp.exp(student - student_max[:, None]) / student_sum[:, None]
                - jnp.exp(target - teacher_max[:, None]) / teacher_sum[:, None]
            )
        ).astype(jnp.bfloat16))
    at_end = (z == 0) | (z == last)
    mean_divergence = lax.psum(jnp.where(at_end, divergence, 0.0), "seq") / total_tokens

    from_low, from_high = [], []
    for s in range(steps):
        send_up = grads[min(s, chunks - 1)]
        send_down = send_up
        if s > 0:
            send_up = jnp.where(z == 0, send_up, from_low[-1])
            send_down = jnp.where(z == last, send_down, from_high[-1])
        from_low.append(lax.ppermute(
            send_up, "seq", [(d, d + 1) for d in range(last) if 0 <= s - d < chunks]))
        from_high.append(lax.ppermute(
            send_down, "seq",
            [(d, d - 1) for d in range(1, seq_count) if 0 <= s - (last - d) < chunks]))
    own = jnp.stack(grads)
    low = lax.dynamic_slice_in_dim(jnp.stack(from_low), jnp.maximum(z - 1, 0), chunks)
    high = lax.dynamic_slice_in_dim(jnp.stack(from_high), jnp.maximum(last - 1 - z, 0), chunks)
    low = jnp.where(z == 0, own, low)
    high = jnp.where(z == last, own, high)
    all_grads = jnp.stack([low, high]).reshape(total_tokens, cols)

    feature = lax.dot_general(
        all_grads, head_weight, (((1,), (1,)), ((), ())), preferred_element_type=jnp.float32
    )
    feature = feature.reshape(2, vocab_count, half, per_dev, rows).transpose(0, 2, 1, 3, 4)
    feature = jnp.concatenate([feature[0], feature[1][::-1]]).reshape(seq_count, own_tokens, rows)
    if vocab_count % seq_count == 0:
        share = vocab_count // seq_count
        out_cols = rows // share
        feature = feature.reshape(seq_count, own_tokens, share, out_cols).transpose(0, 2, 1, 3)
        feature = feature.reshape(vocab_count, own_tokens, out_cols)
        feature = lax.all_to_all(feature, "vocab", split_axis=0, concat_axis=0, tiled=True)
        feature = jnp.sum(feature, axis=0)
        pairs = [
            ((dst * share + b) * seq_count + src, (src * share + b) * seq_count + dst)
            for src in range(seq_count) for dst in range(seq_count) for b in range(share)
        ]
        hidden_grad = lax.ppermute(feature, ("vocab", "seq"), pairs)
    else:
        feature = lax.all_to_all(feature, "seq", split_axis=0, concat_axis=2, tiled=True)
        hidden_grad = lax.psum_scatter(feature[0], "vocab", scatter_dimension=1, tiled=True)
    head_part = lax.dot_general(
        ordered, all_grads, (((0,), (0,)), ((), ())), preferred_element_type=jnp.float32
    )
    return (mean_divergence, hidden_grad, head_part)


def solution(mesh):
    in_specs = (P("seq", None), P("seq", "vocab"), P("seq", "vocab", None))
    out_specs = (P(), P("seq", "vocab"), P("seq", "vocab"))
    return jax.shard_map(body, mesh=mesh, in_specs=in_specs, out_specs=out_specs, check_vma=False)
```

```python
import jax
import jax.numpy as jnp
from jax import lax
from jax.experimental import pallas as pl
from jax.experimental.pallas import tpu as pltpu
from jax.sharding import PartitionSpec as P

LOSS_SCALE = 256.0
VOCAB_TILE = 1024


def after(value, *others):
    return lax.optimization_barrier((value, *others))[0]


def partial_kernel(hidden_ref, head_ref, *out_refs):
    product = lax.dot_general(
        hidden_ref[...], head_ref[...], (((1,), (1,)), ((), ())),
        preferred_element_type=jnp.float32)
    height = out_refs[0].shape[0]
    for i, out_ref in enumerate(out_refs):
        out_ref[...] = product[i * height:(i + 1) * height]


def partial_students(hidden, head_rows, chunk):
    tokens, rows = hidden.shape
    cols = head_rows.shape[0]
    tile = min(VOCAB_TILE, cols)
    count = tokens // chunk
    return pl.pallas_call(
        partial_kernel,
        grid=(pl.cdiv(cols, tile),),
        in_specs=[
            pl.BlockSpec((tokens, rows), lambda i: (0, 0)),
            pl.BlockSpec((tile, rows), lambda i: (i, 0)),
        ],
        out_specs=[pl.BlockSpec((chunk, tile), lambda i: (0, i))] * count,
        out_shape=[jax.ShapeDtypeStruct((chunk, cols), jnp.float32)] * count,
        compiler_params=pltpu.CompilerParams(vmem_limit_bytes=48 * 1024 * 1024),
        cost_estimate=pl.CostEstimate(
            flops=2 * tokens * rows * cols,
            bytes_accessed=2 * rows * cols + 4 * tokens * cols,
            transcendentals=0),
    )(hidden, head_rows)


def body(hidden_states, head_weight, teacher_logits):
    seq_count = lax.axis_size("seq")
    vocab_count = lax.axis_size("vocab")
    half = seq_count // 2
    last = seq_count - 1
    z = lax.axis_index("seq")
    own_tokens, width = hidden_states.shape
    rows, cols = head_weight.shape
    per_dev = teacher_logits.shape[1]
    chunk = half * per_dev
    chunks = vocab_count
    total_tokens = own_tokens * seq_count
    hops = seq_count - 1
    low_side = z < half

    def hop(value, j):
        return lax.ppermute(value, "seq", [(last - j, last - j - 1), (j, j + 1)])

    blocks = [lax.dynamic_slice_in_dim(hidden_states, z * rows, rows, axis=1)]
    for k in range(1, seq_count):
        piece = lax.dynamic_slice_in_dim(
            hidden_states, ((z + k) % seq_count) * rows, rows, axis=1)
        blocks.append(lax.ppermute(
            piece, "seq", [(d, (d + k) % seq_count) for d in range(seq_count)]))
    blocks = jnp.stack(blocks).reshape(seq_count, vocab_count, per_dev, rows)
    sides = []
    for end in (jnp.where(low_side, 0, last), jnp.where(low_side, last, 0)):
        step = jnp.where(end == 0, 1, -1)
        sides.append(jnp.stack(
            [blocks[(z - (end + step * j)) % seq_count] for j in range(half)], axis=1))
    ordered = jnp.stack(sides).reshape(total_tokens, rows)
    head_rows = head_weight.T
    partial = partial_students(ordered, head_rows, chunk)
    own_part, other_part = partial[:chunks], partial[chunks:]

    mine = teacher_logits[0]
    held = [mine] + [
        lax.ppermute(mine, "seq", [(j, 0), (last - j, last)]) for j in range(1, half)
    ]
    held = jnp.concatenate(held, axis=0)
    pieces = jnp.stack([held[:, v * cols:(v + 1) * cols] for v in range(vocab_count)])
    teacher = lax.all_to_all(pieces, "vocab", split_axis=0, concat_axis=0, tiled=True)

    groups = [[i, i + 1] for i in range(0, chunks - 2, 2)] + [[chunks - 2], [chunks - 1]]
    moving = [None] * chunks
    students = [None] * chunks
    gathered = {}
    grads = {}
    travels = {}
    divergence = jnp.zeros((), jnp.float32)
    tie = []

    def send(i, j):
        value = (other_part if j < half else own_part)[i]
        if j > 0:
            value = value + moving[i]
        if tie:
            value = after(value, *tie)
        tie[:] = [value]
        moving[i] = hop(value, j)

    def local_stats(g):
        student = jnp.concatenate([students[i] for i in groups[g]], axis=0)
        target = jnp.concatenate([teacher[i] for i in groups[g]], axis=0).astype(jnp.float32)
        student_top = jnp.max(student, axis=1)
        target_top = jnp.max(target, axis=1)
        target_exp = jnp.exp(target - target_top[:, None])
        stats = jnp.stack([
            student_top,
            target_top,
            jnp.sum(jnp.exp(student - student_top[:, None]), axis=1),
            jnp.sum(target_exp, axis=1),
            jnp.sum(target_exp * (target - student), axis=1),
        ])
        tie.append(stats)
        stats = jnp.broadcast_to(stats, (vocab_count, *stats.shape))
        gathered[g] = lax.all_to_all(stats, "vocab", split_axis=0, concat_axis=0, tiled=True)

    def finish(g):
        stats = gathered[g]
        student = jnp.concatenate([students[i] for i in groups[g]], axis=0)
        target = jnp.concatenate([teacher[i] for i in groups[g]], axis=0).astype(jnp.float32)
        student_max = jnp.max(stats[:, 0], axis=0)
        teacher_max = jnp.max(stats[:, 1], axis=0)
        student_scale = jnp.exp(stats[:, 0] - student_max)
        teacher_scale = jnp.exp(stats[:, 1] - teacher_max)
        student_sum = jnp.sum(stats[:, 2] * student_scale, axis=0)
        teacher_sum = jnp.sum(stats[:, 3] * teacher_scale, axis=0)
        cross = jnp.sum(stats[:, 4] * teacher_scale, axis=0)
        loss = jnp.sum(
            cross / teacher_sum
            - teacher_max
            - jnp.log(teacher_sum)
            + student_max
            + jnp.log(student_sum)
        )
        grads[g] = (
            LOSS_SCALE * (
                jnp.exp(student - student_max[:, None]) / student_sum[:, None]
                - jnp.exp(target - teacher_max[:, None]) / teacher_sum[:, None]
            )
        ).astype(jnp.bfloat16)
        tie.append(grads[g])
        return loss

    ready = {g: max(members) for g, members in enumerate(groups)}
    send(0, 0)
    send(1, 0)
    for s in range(chunks + hops + 6):
        for j in range(1, hops):
            if 0 <= s - (j - 1) < chunks:
                send(s - (j - 1), j)
        if s + 2 < chunks:
            send(s + 2, 0)
        i = s - (hops - 1)
        if 0 <= i < chunks:
            students[i] = own_part[i] + moving[i]
        for g in range(len(groups)):
            if ready[g] == i:
                local_stats(g)
            if ready[g] == i - 1:
                divergence = divergence + finish(g)
    for g in range(len(groups)):
        travels[g] = [grads[g]]
        for j in range(hops):
            travels[g].append(hop(travels[g][-1], j))

    at_end = (z == 0) | (z == last)
    mean_divergence = lax.psum(jnp.where(at_end, divergence, 0.0), "seq") / total_tokens

    near = jnp.minimum(z, last - z)
    first, second = [], []
    for g in range(len(groups)):
        own, other = travels[g][0], travels[g][hops]
        for j in range(1, half):
            own = jnp.where(near == j, travels[g][j], own)
            other = jnp.where(near == j, travels[g][hops - j], other)
        first.append(own)
        second.append(other)
    all_grads = jnp.concatenate(first + second, axis=0)

    feature = jnp.dot(all_grads, head_rows, preferred_element_type=jnp.float32)
    feature = feature.reshape(2, vocab_count, half, per_dev, rows).transpose(0, 2, 1, 3, 4)
    feature = feature.reshape(2, half, own_tokens, rows)
    low = jnp.where(low_side, feature[0], feature[1])
    high = jnp.where(low_side, feature[1], feature[0])
    feature = jnp.concatenate([low, high[::-1]])
    if vocab_count % seq_count == 0:
        share = vocab_count // seq_count
        out_cols = rows // share
        feature = feature.reshape(seq_count, own_tokens, share, out_cols).transpose(0, 2, 1, 3)
        feature = feature.reshape(vocab_count, own_tokens, out_cols)
        feature = lax.all_to_all(feature, "vocab", split_axis=0, concat_axis=0, tiled=True)
        feature = jnp.sum(feature, axis=0)
        pairs = [
            ((dst * share + b) * seq_count + src, (src * share + b) * seq_count + dst)
            for src in range(seq_count) for dst in range(seq_count) for b in range(share)
        ]
        hidden_grad = lax.ppermute(feature, ("vocab", "seq"), pairs)
    else:
        feature = lax.all_to_all(feature, "seq", split_axis=0, concat_axis=2, tiled=True)
        hidden_grad = lax.psum_scatter(feature[0], "vocab", scatter_dimension=1, tiled=True)
    head_part = lax.dot_general(
        all_grads, ordered, (((0,), (0,)), ((), ())), preferred_element_type=jnp.float32
    ).T
    return (mean_divergence, hidden_grad, head_part)


def solution(mesh):
    in_specs = (P("seq", None), P("seq", "vocab"), P("seq", "vocab", None))
    out_specs = (P(), P("seq", "vocab"), P("seq", "vocab"))
    return jax.shard_map(body, mesh=mesh, in_specs=in_specs, out_specs=out_specs, check_vma=False)
```

```python
import jax
import jax.numpy as jnp
from jax import lax
from jax.experimental import pallas as pl
from jax.experimental.pallas import tpu as pltpu
from jax.sharding import PartitionSpec as P

LOSS_SCALE = 256.0
VOCAB_TILE = 1024


def after(value, *others):
    return lax.optimization_barrier((value, *others))[0]


def partial_kernel(hidden_ref, head_ref, *out_refs):
    product = lax.dot_general(
        hidden_ref[...], head_ref[...], (((1,), (1,)), ((), ())),
        preferred_element_type=jnp.float32)
    height = out_refs[0].shape[0]
    for i, out_ref in enumerate(out_refs):
        out_ref[...] = product[i * height:(i + 1) * height]


def partial_students(hidden, head_rows, chunk):
    tokens, rows = hidden.shape
    cols = head_rows.shape[0]
    tile = min(VOCAB_TILE, cols)
    count = tokens // chunk
    return pl.pallas_call(
        partial_kernel,
        grid=(pl.cdiv(cols, tile),),
        in_specs=[
            pl.BlockSpec((tokens, rows), lambda i: (0, 0)),
            pl.BlockSpec((tile, rows), lambda i: (i, 0)),
        ],
        out_specs=[pl.BlockSpec((chunk, tile), lambda i: (0, i))] * count,
        out_shape=[jax.ShapeDtypeStruct((chunk, cols), jnp.float32)] * count,
        compiler_params=pltpu.CompilerParams(vmem_limit_bytes=48 * 1024 * 1024),
        cost_estimate=pl.CostEstimate(
            flops=2 * tokens * rows * cols,
            bytes_accessed=2 * rows * cols + 4 * tokens * cols,
            transcendentals=0),
    )(hidden, head_rows)


def body(hidden_states, head_weight, teacher_logits):
    seq_count = lax.axis_size("seq")
    vocab_count = lax.axis_size("vocab")
    half = seq_count // 2
    last = seq_count - 1
    z = lax.axis_index("seq")
    own_tokens, width = hidden_states.shape
    rows, cols = head_weight.shape
    per_dev = teacher_logits.shape[1]
    chunk = half * per_dev
    chunks = vocab_count
    total_tokens = own_tokens * seq_count
    hops = seq_count - 1
    low_side = z < half

    def hop(value, j):
        return lax.ppermute(value, "seq", [(last - j, last - j - 1), (j, j + 1)])

    blocks = [lax.dynamic_slice_in_dim(hidden_states, z * rows, rows, axis=1)]
    for k in range(1, seq_count):
        piece = lax.dynamic_slice_in_dim(
            hidden_states, ((z + k) % seq_count) * rows, rows, axis=1)
        blocks.append(lax.ppermute(
            piece, "seq", [(d, (d + k) % seq_count) for d in range(seq_count)]))
    blocks = jnp.stack(blocks).reshape(seq_count, vocab_count, per_dev, rows)
    sides = []
    for end in (jnp.where(low_side, 0, last), jnp.where(low_side, last, 0)):
        step = jnp.where(end == 0, 1, -1)
        sides.append(jnp.stack(
            [blocks[(z - (end + step * j)) % seq_count] for j in range(half)], axis=1))
    ordered = jnp.stack(sides).reshape(total_tokens, rows)
    head_rows = head_weight.T
    half_tokens = total_tokens // 2

    mine, ordered = lax.optimization_barrier((teacher_logits[0], ordered))
    held = [mine] + [
        lax.ppermute(mine, "seq", [(j, 0), (last - j, last)]) for j in range(1, half)
    ]
    held = jnp.concatenate(held, axis=0)

    groups = [[i, i + 1] for i in range(0, chunks - 2, 2)] + [[chunks - 2], [chunks - 1]]
    moving = [None] * chunks
    students = [None] * chunks
    targets = []
    gathered = {}
    travels = {}
    losses = []
    tie = []

    def tied(value):
        value = after(value, *tie) if tie else value
        tie[:] = [value]
        return value

    def send(i, j):
        part = (other_part if j < half else own_part)[i]
        if j == 0:
            value = tied(part)
        else:
            value = part + tied(moving[i])
            tie[:] = [value]
        moving[i] = hop(value, j)

    def exchange_teacher():
        rows_held = tied(held)
        pieces = jnp.stack([rows_held[:, v * cols:(v + 1) * cols] for v in range(vocab_count)])
        tie[:] = [pieces]
        targets.extend(
            lax.all_to_all(pieces, "vocab", split_axis=0, concat_axis=0, tiled=True))

    def group_rows(g):
        student = jnp.concatenate([students[i] for i in groups[g]], axis=0)
        target = jnp.concatenate([targets[i] for i in groups[g]], axis=0)
        return student, target.astype(jnp.float32)

    def local_stats(g):
        student, target = group_rows(g)
        student_top = jnp.max(student, axis=1)
        target_top = jnp.max(target, axis=1)
        target_exp = jnp.exp(target - target_top[:, None])
        stats = jnp.stack([
            student_top,
            target_top,
            jnp.sum(jnp.exp(student - student_top[:, None]), axis=1),
            jnp.sum(target_exp, axis=1),
            jnp.sum(target_exp * (target - student), axis=1),
        ])
        tie[:] = [stats]
        stats = jnp.broadcast_to(stats, (vocab_count, *stats.shape))
        gathered[g] = lax.all_to_all(stats, "vocab", split_axis=0, concat_axis=0, tiled=True)

    def finish(g):
        stats = tied(gathered[g])
        student, target = group_rows(g)
        student_max = jnp.max(stats[:, 0], axis=0)
        teacher_max = jnp.max(stats[:, 1], axis=0)
        student_scale = jnp.exp(stats[:, 0] - student_max)
        teacher_scale = jnp.exp(stats[:, 1] - teacher_max)
        student_sum = jnp.sum(stats[:, 2] * student_scale, axis=0)
        teacher_sum = jnp.sum(stats[:, 3] * teacher_scale, axis=0)
        cross = jnp.sum(stats[:, 4] * teacher_scale, axis=0)
        losses.append(jnp.stack([cross, teacher_sum, teacher_max, student_max, student_sum]))
        grad = (
            LOSS_SCALE * (
                jnp.exp(student - student_max[:, None]) / student_sum[:, None]
                - jnp.exp(target - teacher_max[:, None]) / teacher_sum[:, None]
            )
        ).astype(jnp.bfloat16)
        tie[:] = [grad]
        travels[g] = [grad]

    def send_grad(g, j):
        value = travels[g][j] if j == 0 else tied(travels[g][j])
        travels[g].append(hop(value, j))

    lag = 2
    sums_end = chunks - 1 + lag * (hops - 1)
    slots = {}

    def plan(slot, order, call, *args):
        slots.setdefault(slot, []).append((order, len(slots[slot]) if slot in slots else 0, call, args))

    for i in range(chunks):
        for j in range(hops):
            plan(i + lag * j, j, send, i, j)
    plan(1, 50, exchange_teacher)
    for g, members in enumerate(groups):
        arrived = max(members) + lag * hops
        plan(arrived, 20, local_stats, g)
        slot = arrived + 1
        plan(slot, 30, finish, g)
        for j in range(hops):
            plan(slot, 40 + j, send_grad, g, j)
            slot += lag if slot < sums_end else 1

    def sum_up(i):
        students[i] = own_part[i] + tied(moving[i])
        tie[:] = [students[i]]

    for i in range(chunks):
        plan(i + lag * hops, 10, sum_up, i)

    partial = partial_students(ordered[half_tokens:], head_rows, chunk)
    other_part = list(partial)
    own_part = None
    for slot in sorted(slots):
        for _, _, call, args in sorted(slots[slot], key=lambda e: e[:2]):
            call(*args)
        if own_part is None:
            own_part = list(partial_students(tied(ordered[:half_tokens]), head_rows, chunk))
            tie[:] = [own_part[0]]

    cross, teacher_sum, teacher_max, student_max, student_sum = jnp.concatenate(losses, axis=1)
    divergence = jnp.sum(
        cross / teacher_sum
        - teacher_max
        - jnp.log(teacher_sum)
        + student_max
        + jnp.log(student_sum)
    )
    at_end = (z == 0) | (z == last)
    divergence = tied(jnp.where(at_end, divergence, 0.0))
    mean_divergence = lax.psum(divergence, "seq") / total_tokens
    tie[:] = [mean_divergence]

    near = jnp.minimum(z, last - z)
    first, second = [], []
    for g in range(len(groups)):
        own, other = travels[g][0], travels[g][hops]
        for j in range(1, half):
            own = jnp.where(near == j, travels[g][j], own)
            other = jnp.where(near == j, travels[g][hops - j], other)
        first.append(own)
        second.append(other)
    early = len(groups) - 2
    early_rows = sum(len(members) for members in groups[:early]) * chunk
    early_grads = jnp.concatenate(first[:early] + second[:early], axis=0)
    late_grads = jnp.concatenate(first[early:] + second[early:], axis=0)
    feature_early = jnp.dot(early_grads, head_rows, preferred_element_type=jnp.float32)
    late_grads = tied(late_grads)
    feature_late = jnp.dot(late_grads, head_rows, preferred_element_type=jnp.float32)
    feature = jnp.concatenate(
        [feature_early.reshape(2, -1, rows), feature_late.reshape(2, -1, rows)], axis=1)
    both = ordered.reshape(2, half_tokens, rows)
    matching = jnp.concatenate([
        both[:, :early_rows].reshape(-1, rows), both[:, early_rows:].reshape(-1, rows)])
    all_grads = jnp.concatenate([early_grads, late_grads])
    feature = feature.reshape(2, vocab_count, half, per_dev, rows).transpose(0, 2, 1, 3, 4)
    feature = feature.reshape(2, half, own_tokens, rows)
    low = jnp.where(low_side, feature[0], feature[1])
    high = jnp.where(low_side, feature[1], feature[0])
    feature = jnp.concatenate([low, high[::-1]])
    if vocab_count % seq_count == 0:
        share = vocab_count // seq_count
        out_cols = rows // share
        feature = feature.reshape(seq_count, own_tokens, share, out_cols).transpose(0, 2, 1, 3)
        feature = feature.reshape(vocab_count, own_tokens, out_cols)
        feature = lax.all_to_all(feature, "vocab", split_axis=0, concat_axis=0, tiled=True)
        feature = jnp.sum(feature, axis=0)
        pairs = [
            ((dst * share + b) * seq_count + src, (src * share + b) * seq_count + dst)
            for src in range(seq_count) for dst in range(seq_count) for b in range(share)
        ]
        hidden_grad = lax.ppermute(feature, ("vocab", "seq"), pairs)
    else:
        feature = lax.all_to_all(feature, "seq", split_axis=0, concat_axis=2, tiled=True)
        hidden_grad = lax.psum_scatter(feature[0], "vocab", scatter_dimension=1, tiled=True)
    head_part = lax.dot_general(
        all_grads, matching, (((0,), (0,)), ((), ())), preferred_element_type=jnp.float32
    ).T
    return (mean_divergence, hidden_grad, head_part)


def solution(mesh):
    in_specs = (P("seq", None), P("seq", "vocab"), P("seq", "vocab", None))
    out_specs = (P(), P("seq", "vocab"), P("seq", "vocab"))
    return jax.shard_map(body, mesh=mesh, in_specs=in_specs, out_specs=out_specs, check_vma=False)
```

```python
import jax
import jax.numpy as jnp
from jax import lax
from jax.experimental import pallas as pl
from jax.experimental.pallas import tpu as pltpu
from jax.sharding import PartitionSpec as P

LOSS_SCALE = 256.0
VOCAB_TILE = 1024


def after(value, *others):
    return lax.optimization_barrier((value, *others))[0]


def partial_kernel(hidden_ref, head_ref, *out_refs):
    product = jnp.dot(head_ref[...], hidden_ref[...], preferred_element_type=jnp.float32).T
    height = out_refs[0].shape[0]
    for i, out_ref in enumerate(out_refs):
        out_ref[...] = product[i * height:(i + 1) * height]


def partial_students(hidden, head_rows, chunk):
    tokens, rows = hidden.shape
    cols = head_rows.shape[0]
    tile = min(VOCAB_TILE, cols)
    count = tokens // chunk
    return pl.pallas_call(
        partial_kernel,
        grid=(pl.cdiv(cols, tile),),
        in_specs=[
            pl.BlockSpec((rows, tokens), lambda i: (0, 0)),
            pl.BlockSpec((tile, rows), lambda i: (i, 0)),
        ],
        out_specs=[pl.BlockSpec((chunk, tile), lambda i: (0, i))] * count,
        out_shape=[jax.ShapeDtypeStruct((chunk, cols), jnp.float32)] * count,
        compiler_params=pltpu.CompilerParams(vmem_limit_bytes=48 * 1024 * 1024),
        cost_estimate=pl.CostEstimate(
            flops=2 * tokens * rows * cols,
            bytes_accessed=2 * rows * cols + 4 * tokens * cols,
            transcendentals=0),
    )(hidden.T, head_rows)


def body(hidden_states, head_weight, teacher_logits):
    seq_count = lax.axis_size("seq")
    vocab_count = lax.axis_size("vocab")
    half = seq_count // 2
    last = seq_count - 1
    z = lax.axis_index("seq")
    own_tokens, width = hidden_states.shape
    rows, cols = head_weight.shape
    per_dev = teacher_logits.shape[1]
    chunk = half * per_dev
    chunks = vocab_count
    total_tokens = own_tokens * seq_count
    hops = seq_count - 1
    low_side = z < half

    def hop(value, j):
        return lax.ppermute(value, "seq", [(last - j, last - j - 1), (j, j + 1)])

    blocks = [lax.dynamic_slice_in_dim(hidden_states, z * rows, rows, axis=1)]
    for k in range(1, seq_count):
        piece = lax.dynamic_slice_in_dim(
            hidden_states, ((z + k) % seq_count) * rows, rows, axis=1)
        blocks.append(lax.ppermute(
            piece, "seq", [(d, (d + k) % seq_count) for d in range(seq_count)]))
    blocks = jnp.stack(blocks).reshape(seq_count, vocab_count, per_dev, rows)
    sides = []
    for end in (jnp.where(low_side, 0, last), jnp.where(low_side, last, 0)):
        step = jnp.where(end == 0, 1, -1)
        sides.append(jnp.stack(
            [blocks[(z - (end + step * j)) % seq_count] for j in range(half)], axis=1))
    ordered = jnp.stack(sides).reshape(total_tokens, rows)
    head_rows = head_weight.T
    half_tokens = total_tokens // 2

    mine, ordered = lax.optimization_barrier((teacher_logits[0], ordered))
    held = [mine] + [
        lax.ppermute(mine, "seq", [(j, 0), (last - j, last)]) for j in range(1, half)
    ]
    held = jnp.concatenate(held, axis=0)

    groups = [list(range(i, min(i + 3, chunks - 2))) for i in range(0, chunks - 2, 3)]
    groups.append([chunks - 2, chunks - 1])
    loads = [[members] for members in groups[:-1]] + [[[i] for i in groups[-1]]]
    moving = [None] * chunks
    students = [None] * chunks
    targets = []
    gathered = {}
    travels = {}
    losses = []
    tie = []

    def tied(value):
        value = after(value, *tie) if tie else value
        tie[:] = [value]
        return value

    def send(i, j):
        part = (other_part if j < half else own_part)[i]
        if j == 0:
            value = tied(part)
        else:
            value = part + tied(moving[i])
            tie[:] = [value]
        moving[i] = hop(value, j)

    def exchange_teacher():
        rows_held = tied(held)
        pieces = jnp.stack([rows_held[:, v * cols:(v + 1) * cols] for v in range(vocab_count)])
        tie[:] = [pieces]
        targets.extend(
            lax.all_to_all(pieces, "vocab", split_axis=0, concat_axis=0, tiled=True))

    def rows_of(members):
        student = jnp.concatenate([students[i] for i in members], axis=0)
        target = jnp.concatenate([targets[i] for i in members], axis=0)
        return student, target.astype(jnp.float32)

    def local_stats(g):
        student, target = rows_of(groups[g])
        student_top = jnp.max(student, axis=1)
        target_top = jnp.max(target, axis=1)
        target_exp = jnp.exp(target - target_top[:, None])
        stats = jnp.stack([
            student_top,
            target_top,
            jnp.sum(jnp.exp(student - student_top[:, None]), axis=1),
            jnp.sum(target_exp, axis=1),
            jnp.sum(target_exp * (target - student), axis=1),
        ])
        tie[:] = [stats]
        stats = jnp.broadcast_to(stats, (vocab_count, *stats.shape))
        gathered[g] = lax.all_to_all(stats, "vocab", split_axis=0, concat_axis=0, tiled=True)

    def finish(g):
        stats = tied(gathered[g])
        student_max = jnp.max(stats[:, 0], axis=0)
        teacher_max = jnp.max(stats[:, 1], axis=0)
        student_scale = jnp.exp(stats[:, 0] - student_max)
        teacher_scale = jnp.exp(stats[:, 1] - teacher_max)
        student_sum = jnp.sum(stats[:, 2] * student_scale, axis=0)
        teacher_sum = jnp.sum(stats[:, 3] * teacher_scale, axis=0)
        cross = jnp.sum(stats[:, 4] * teacher_scale, axis=0)
        losses.append(jnp.stack([cross, teacher_sum, teacher_max, student_max, student_sum]))
        start = 0
        for p, members in enumerate(loads[g]):
            student, target = rows_of(members)
            at = slice(start, start + len(members) * chunk)
            start = at.stop
            grad = (
                LOSS_SCALE * (
                    jnp.exp(student - student_max[at, None]) / student_sum[at, None]
                    - jnp.exp(target - teacher_max[at, None]) / teacher_sum[at, None]
                )
            ).astype(jnp.bfloat16)
            tie[:] = [grad]
            travels[g, p] = [grad]

    def send_grad(g, p, j):
        value = travels[g, p][j] if j == 0 else tied(travels[g, p][j])
        travels[g, p].append(hop(value, j))

    def sum_up(i):
        students[i] = own_part[i] + tied(moving[i])
        tie[:] = [students[i]]

    def loss():
        cross, teacher_sum, teacher_max, student_max, student_sum = tied(
            jnp.concatenate(losses, axis=1))
        divergence = jnp.sum(
            cross / teacher_sum
            - teacher_max
            - jnp.log(teacher_sum)
            + student_max
            + jnp.log(student_sum)
        )
        at_end = (z == 0) | (z == last)
        total = lax.psum(jnp.where(at_end, divergence, 0.0), "seq")
        tie[:] = [total]
        return total / total_tokens

    near = jnp.minimum(z, last - z)

    def arrived(keys):
        first, second = [], []
        for key in keys:
            own, other = travels[key][0], travels[key][hops]
            for j in range(1, half):
                own = jnp.where(near == j, travels[key][j], own)
                other = jnp.where(near == j, travels[key][hops - j], other)
            first.append(own)
            second.append(other)
        return jnp.concatenate(first + second, axis=0)

    slots = {}

    def plan(slot, order, call, *args):
        slots.setdefault(slot, []).append((order, len(slots.get(slot, ())), call, args))

    for i in range(chunks):
        plan(i - 1, 5, send, i, 0)
        for j in range(1, hops):
            plan(i + j, j, send, i, j)
        plan(i + hops, 4, sum_up, i)
    plan(1, 50, exchange_teacher)
    keys = []
    for g, members in enumerate(groups):
        slot = max(members) + hops
        plan(slot, 20, local_stats, g)
        slot += 1
        plan(slot, 30, finish, g)
        for p in range(len(loads[g])):
            keys.append((g, p))
            at = slot
            for j in range(hops):
                plan(at, 40 + j, send_grad, g, p, j)
                at += 2 if at < chunks + hops else 1

    other_part = list(partial_students(ordered[half_tokens:], head_rows, chunk))
    own_part = None
    final = max(slots)
    early_keys = [key for key in keys if key[0] < len(groups) - 1]
    late_keys = [key for key in keys if key[0] == len(groups) - 1]
    for slot in sorted(slots):
        if slot == final:
            mean_divergence = loss()
        for _, _, call, args in sorted(slots[slot], key=lambda e: e[:2]):
            call(*args)
        if own_part is None:
            own_part = list(partial_students(tied(ordered[:half_tokens]), head_rows, chunk))
            tie[:] = [own_part[0]]

    early_grads = tied(arrived(early_keys))
    feature_early = jnp.dot(early_grads, head_rows, preferred_element_type=jnp.float32)
    tie[:] = [feature_early]
    late_grads = tied(arrived(late_keys))
    feature_late = jnp.dot(late_grads, head_rows, preferred_element_type=jnp.float32)
    early_rows = early_grads.shape[0] // 2
    feature = jnp.concatenate(
        [feature_early.reshape(2, -1, rows), feature_late.reshape(2, -1, rows)], axis=1)
    both = ordered.reshape(2, half_tokens, rows)
    matching = jnp.concatenate([
        both[:, :early_rows].reshape(-1, rows), both[:, early_rows:].reshape(-1, rows)])
    all_grads = jnp.concatenate([early_grads, late_grads])
    head_part = lax.dot_general(
        all_grads, matching, (((0,), (0,)), ((), ())), preferred_element_type=jnp.float32
    ).T
    feature = feature.reshape(2, vocab_count, half, per_dev, rows).transpose(0, 2, 1, 3, 4)
    feature = feature.reshape(2, half, own_tokens, rows)
    low = jnp.where(low_side, feature[0], feature[1])
    high = jnp.where(low_side, feature[1], feature[0])
    feature = jnp.concatenate([low, high[::-1]])
    if vocab_count % seq_count == 0:
        share = vocab_count // seq_count
        out_cols = rows // share
        feature = feature.reshape(seq_count, own_tokens, share, out_cols).transpose(0, 2, 1, 3)
        feature = feature.reshape(vocab_count, own_tokens, out_cols)
        feature = lax.all_to_all(feature, "vocab", split_axis=0, concat_axis=0, tiled=True)
        feature, head_part = lax.optimization_barrier((feature, head_part))
        feature = jnp.sum(feature, axis=0)
        pairs = [
            ((dst * share + b) * seq_count + src, (src * share + b) * seq_count + dst)
            for src in range(seq_count) for dst in range(seq_count) for b in range(share)
        ]
        hidden_grad = lax.ppermute(feature, ("vocab", "seq"), pairs)
    else:
        feature = lax.all_to_all(feature, "seq", split_axis=0, concat_axis=2, tiled=True)
        hidden_grad = lax.psum_scatter(feature[0], "vocab", scatter_dimension=1, tiled=True)
    return (mean_divergence, hidden_grad, head_part)


def solution(mesh):
    in_specs = (P("seq", None), P("seq", "vocab"), P("seq", "vocab", None))
    out_specs = (P(), P("seq", "vocab"), P("seq", "vocab"))
    return jax.shard_map(body, mesh=mesh, in_specs=in_specs, out_specs=out_specs, check_vma=False)
```

```python
import jax
import jax.numpy as jnp
from jax import lax
from jax.experimental import pallas as pl
from jax.experimental.pallas import tpu as pltpu
from jax.sharding import PartitionSpec as P

LOSS_SCALE = 256.0
VOCAB_TILE = 1024


def after(value, *others):
    return lax.optimization_barrier((value, *others))[0]


def partial_kernel(hidden_ref, head_ref, *out_refs):
    product = lax.dot_general(
        hidden_ref[...], head_ref[...], (((1,), (1,)), ((), ())),
        preferred_element_type=jnp.float32)
    height = out_refs[0].shape[0]
    for i, out_ref in enumerate(out_refs):
        out_ref[...] = product[i * height:(i + 1) * height]


def partial_students(hidden, head_rows, chunk):
    tokens, rows = hidden.shape
    cols = head_rows.shape[0]
    tile = min(VOCAB_TILE, cols)
    count = tokens // chunk
    return pl.pallas_call(
        partial_kernel,
        grid=(pl.cdiv(cols, tile),),
        in_specs=[
            pl.BlockSpec((tokens, rows), lambda i: (0, 0)),
            pl.BlockSpec((tile, rows), lambda i: (i, 0)),
        ],
        out_specs=[pl.BlockSpec((chunk, tile), lambda i: (0, i))] * count,
        out_shape=[jax.ShapeDtypeStruct((chunk, cols), jnp.float32)] * count,
        compiler_params=pltpu.CompilerParams(vmem_limit_bytes=16 * 1024 * 1024),
        cost_estimate=pl.CostEstimate(
            flops=2 * tokens * rows * cols,
            bytes_accessed=2 * rows * cols + 4 * tokens * cols,
            transcendentals=0),
    )(hidden, head_rows)


def body(hidden_states, head_weight, teacher_logits):
    seq_count = lax.axis_size("seq")
    vocab_count = lax.axis_size("vocab")
    half = seq_count // 2
    last = seq_count - 1
    z = lax.axis_index("seq")
    own_tokens, width = hidden_states.shape
    rows, cols = head_weight.shape
    per_dev = teacher_logits.shape[1]
    chunk = half * per_dev
    chunks = vocab_count
    total_tokens = own_tokens * seq_count
    hops = seq_count - 1
    low_side = z < half

    def hop(value, j):
        return lax.ppermute(value, "seq", [(last - j, last - j - 1), (j, j + 1)])

    strips = [
        lax.dynamic_slice_in_dim(hidden_states, ((z + k) % seq_count) * rows, rows, axis=1)
        for k in range(seq_count)
    ]
    blocks = [strips[0]] + [
        lax.ppermute(strips[k], "seq", [(d, (d + k) % seq_count) for d in range(seq_count)])
        for k in range(1, seq_count)
    ]
    blocks = jnp.stack(blocks).reshape(seq_count, vocab_count, per_dev, rows)
    sides = []
    for end in (jnp.where(low_side, 0, last), jnp.where(low_side, last, 0)):
        step = jnp.where(end == 0, 1, -1)
        sides.append(jnp.stack(
            [blocks[(z - (end + step * j)) % seq_count] for j in range(half)], axis=1))
    ordered = jnp.stack(sides).reshape(total_tokens, rows)
    head_rows = head_weight.T
    half_tokens = total_tokens // 2

    mine, ordered = lax.optimization_barrier((teacher_logits[0], ordered))
    held = [mine] + [
        lax.ppermute(mine, "seq", [(j, 0), (last - j, last)]) for j in range(1, half)
    ]

    middle = chunks // 2
    groups = [list(range(middle)), list(range(middle, chunks))]
    loads = [[[i, i + 1] for i in range(0, middle - 1, 2)] + [[middle - 1]] * (middle % 2),
             [[middle, middle + 1]] + [[i] for i in range(middle + 2, chunks)]]
    moving = [None] * chunks
    students = [None] * chunks
    targets = []
    pieces = []
    locals_ = [None] * chunks
    exchanged = {}
    travels = {}
    settled_loss = []
    tie = []

    def tied(value):
        value = after(value, *tie) if tie else value
        tie[:] = [value]
        return value

    def send(i, j):
        part = (other_part if j < half else own_part)[i]
        if j == 0:
            value = tied(part)
        else:
            value = part + tied(moving[i])
            tie[:] = [value]
        moving[i] = hop(value, j)

    def cut_teacher():
        rows_held = tied(jnp.concatenate(held, axis=0))
        pieces.append(jnp.stack(
            [rows_held[:, v * cols:(v + 1) * cols] for v in range(vocab_count)]))
        tie[:] = pieces

    def exchange_teacher():
        targets.extend(
            lax.all_to_all(tied(pieces[0]), "vocab", split_axis=0, concat_axis=0, tiled=True))

    def hold_teacher():
        held[:] = lax.optimization_barrier((*held, *tie))[:half]
        tie[:] = [held[-1]]

    def local_stats(i):
        student = tied(students[i])
        target = targets[i].astype(jnp.float32)
        student_top = jnp.max(student, axis=1)
        target_top = jnp.max(target, axis=1)
        target_exp = jnp.exp(target - target_top[:, None])
        locals_[i] = jnp.stack([
            student_top,
            target_top,
            jnp.sum(jnp.exp(student - student_top[:, None]), axis=1),
            jnp.sum(target_exp, axis=1),
            jnp.sum(target_exp * (target - student), axis=1),
        ])
        tie[:] = [locals_[i]]

    def exchange_stats(g):
        stats = jnp.concatenate([locals_[i] for i in groups[g]], axis=1)
        tie[:] = [stats]
        stats = jnp.broadcast_to(stats, (vocab_count, *stats.shape))
        stats = lax.all_to_all(stats, "vocab", split_axis=0, concat_axis=0, tiled=True)
        exchanged[g] = stats

    def merge_stats(g):
        stats = tied(exchanged[g])
        student_max = jnp.max(stats[:, 0], axis=0)
        teacher_max = jnp.max(stats[:, 1], axis=0)
        student_scale = jnp.exp(stats[:, 0] - student_max)
        teacher_scale = jnp.exp(stats[:, 1] - teacher_max)
        student_sum = jnp.sum(stats[:, 2] * student_scale, axis=0)
        teacher_sum = jnp.sum(stats[:, 3] * teacher_scale, axis=0)
        cross = jnp.sum(stats[:, 4] * teacher_scale, axis=0)
        exchanged[g] = lax.optimization_barrier(
            (student_max, student_sum, teacher_max, teacher_sum, cross))
        tie[:] = [exchanged[g][0]]

    def form_grads(g, p):
        student_max, student_sum, teacher_max, teacher_sum, _ = exchanged[g]
        grads = []
        for i in loads[g][p]:
            first = (i - groups[g][0]) * chunk
            at = slice(first, first + chunk)
            student = tied(students[i])
            target = targets[i].astype(jnp.float32)
            grads.append((
                LOSS_SCALE * (
                    jnp.exp(student - student_max[at, None]) / student_sum[at, None]
                    - jnp.exp(target - teacher_max[at, None]) / teacher_sum[at, None]
                )
            ).astype(jnp.bfloat16))
        grad = jnp.concatenate(grads, axis=0)
        tie[:] = [grad]
        travels[g, p] = [grad]

    def send_grad(g, p, j):
        value = travels[g, p][j] if j == 0 else tied(travels[g, p][j])
        travels[g, p].append(hop(value, j))

    def sum_up(i):
        students[i] = own_part[i] + tied(moving[i])
        tie[:] = [students[i]]

    def loss():
        student_max, student_sum, teacher_max, teacher_sum, cross = (
            jnp.concatenate(both) for both in zip(*exchanged.values()))
        divergence = jnp.sum(
            cross / teacher_sum
            - teacher_max
            - jnp.log(teacher_sum)
            + student_max
            + jnp.log(student_sum)
        )
        travels["loss"] = [tied(divergence.reshape(1, 1))]

    def send_loss(j):
        value = travels["loss"][j] if j == 0 else tied(travels["loss"][j])
        travels["loss"].append(hop(value, j))

    near = jnp.minimum(z, last - z)

    def settle(key):
        own, other = travels[key][0], travels[key][hops]
        for j in range(1, half):
            own = jnp.where(near == j, travels[key][j], own)
            other = jnp.where(near == j, travels[key][hops - j], other)
        return own, other

    def settled(keys):
        pairs = [settle(key) for key in keys]
        return jnp.concatenate([p[0] for p in pairs] + [p[1] for p in pairs], axis=0)

    features = []

    def settle_loss():
        travels["loss"][hops] = tied(travels["loss"][hops])
        settled_loss.append(sum(settle("loss"))[0, 0] / total_tokens)
        tie[:] = [settled_loss[0]]

    def early_feature():
        grads = tied(settled(early_keys))
        features.append((grads, jnp.dot(grads, head_rows, preferred_element_type=jnp.float32)))
        tie[:] = [features[0][1]]

    slots = {}

    def plan(slot, order, call, *args):
        slots.setdefault(slot, []).append((order, len(slots.get(slot, ())), call, args))

    for i in range(chunks):
        plan(i - 1, 5, send, i, 0)
        for j in range(1, hops):
            plan(i + j, j, send, i, j)
        plan(i + hops, 4, sum_up, i)
    end = chunks + hops - 1
    plan(2, 0, hold_teacher)
    plan(3, 15, cut_teacher)
    plan(4, 15, exchange_teacher)
    stats_slot = middle + hops
    for i in range(chunks):
        wait = min(6 + i // 2, stats_slot) if i < middle else i + hops + (i == middle)
        plan(max(i + hops, wait), 15, local_stats, i)
    early_keys, late_keys = [], []
    for g, slot in enumerate((stats_slot, end)):
        plan(slot, 18, exchange_stats, g)
        plan(slot + 1, 20, merge_stats, g)
        for p in range(len(loads[g])):
            (late_keys if g else early_keys).append((g, p))
            first = slot + 1 + (0 if g else p)
            plan(first, 40 + 2 * p, form_grads, g, p)
            plan(first, 41 + 2 * p, send_grad, g, p, 0)
            for j in range(1, hops):
                if g == 0:
                    plan(first + j, 30 - j if first + j <= end else 90 - j, send_grad, g, p, j)
                else:
                    plan(first + j + (p + 1) // 2, 120 + 10 * j + p, send_grad, g, p, j)
    plan(end + 1, 60, loss)
    for j in range(hops):
        plan(end + 1 + j + (j > 0), 1510, send_loss, j)
    final = max(slots)
    plan(final, 1600, early_feature)
    plan(final, 1700, settle_loss)

    first_part = jnp.dot(
        ordered[half_tokens:half_tokens + chunk], head_weight, preferred_element_type=jnp.float32)
    other_part = [first_part]
    own_part = None
    for slot in sorted(slots):
        for _, _, call, args in sorted(slots[slot], key=lambda e: e[:2]):
            call(*args)
        if own_part is None:
            remaining = tied(jnp.concatenate(
                [ordered[half_tokens + chunk:], ordered[:half_tokens]]))
            parts = partial_students(remaining, head_rows, chunk)
            other_part.extend(parts[:chunks - 1])
            own_part = parts[chunks - 1:]
            tie[:] = [own_part[0]]

    mean_divergence = settled_loss[0]
    early_grads, feature_early = features[0]
    for key in late_keys:
        travels[key][hops] = tied(travels[key][hops])
    late_grads = settled(late_keys)
    feature_late = jnp.dot(late_grads, head_rows, preferred_element_type=jnp.float32)
    early_rows = early_grads.shape[0] // 2
    feature = jnp.concatenate(
        [feature_early.reshape(2, -1, rows), feature_late.reshape(2, -1, rows)], axis=1)
    both = ordered.reshape(2, half_tokens, rows)
    matching = jnp.concatenate([
        both[:, :early_rows].reshape(-1, rows), both[:, early_rows:].reshape(-1, rows)])
    all_grads = jnp.concatenate([early_grads, late_grads])
    head_part = lax.dot_general(
        all_grads, matching, (((0,), (0,)), ((), ())), preferred_element_type=jnp.float32
    ).T
    feature = feature.reshape(2, vocab_count, half, per_dev, rows).transpose(0, 2, 1, 3, 4)
    feature = feature.reshape(2, half, own_tokens, rows)
    low = jnp.where(low_side, feature[0], feature[1])
    high = jnp.where(low_side, feature[1], feature[0])
    feature = jnp.concatenate([low, high[::-1]])
    if vocab_count % seq_count == 0:
        share = vocab_count // seq_count
        out_cols = rows // share
        feature = feature.reshape(seq_count, own_tokens, share, out_cols).transpose(0, 2, 1, 3)
        feature = feature.reshape(vocab_count, own_tokens, out_cols)
        feature = lax.all_to_all(feature, "vocab", split_axis=0, concat_axis=0, tiled=True)
        feature, head_part = lax.optimization_barrier((feature, head_part))
        feature = jnp.sum(feature, axis=0)
        pairs = [
            ((dst * share + b) * seq_count + src, (src * share + b) * seq_count + dst)
            for src in range(seq_count) for dst in range(seq_count) for b in range(share)
        ]
        hidden_grad = lax.ppermute(feature, ("vocab", "seq"), pairs)
    else:
        feature = lax.all_to_all(feature, "seq", split_axis=0, concat_axis=2, tiled=True)
        hidden_grad = lax.psum_scatter(feature[0], "vocab", scatter_dimension=1, tiled=True)
    return (mean_divergence, hidden_grad, head_part)


def solution(mesh):
    in_specs = (P("seq", None), P("seq", "vocab"), P("seq", "vocab", None))
    out_specs = (P(), P("seq", "vocab"), P("seq", "vocab"))
    return jax.shard_map(body, mesh=mesh, in_specs=in_specs, out_specs=out_specs, check_vma=False)
```

```python
import functools

import jax
import jax.numpy as jnp
from jax import lax
from jax.experimental import pallas as pl
from jax.experimental.pallas import tpu as pltpu
from jax.sharding import PartitionSpec as P

LOSS_SCALE = 256.0
VOCAB_TILE = 1024


def after(value, *others):
    return lax.optimization_barrier((value, *others))[0]


def partial_kernel(hidden_ref, head_ref, *out_refs):
    product = lax.dot_general(
        hidden_ref[...], head_ref[...], (((1,), (1,)), ((), ())),
        preferred_element_type=jnp.float32)
    height = out_refs[0].shape[0]
    for i, out_ref in enumerate(out_refs):
        out_ref[...] = product[i * height:(i + 1) * height]


def partial_students(hidden, head_rows, chunk):
    tokens, rows = hidden.shape
    cols = head_rows.shape[0]
    tile = min(VOCAB_TILE, cols)
    count = tokens // chunk
    return pl.pallas_call(
        partial_kernel,
        grid=(pl.cdiv(cols, tile),),
        in_specs=[
            pl.BlockSpec((tokens, rows), lambda i: (0, 0)),
            pl.BlockSpec((tile, rows), lambda i: (i, 0)),
        ],
        out_specs=[pl.BlockSpec((chunk, tile), lambda i: (0, i))] * count,
        out_shape=[jax.ShapeDtypeStruct((chunk, cols), jnp.float32)] * count,
        compiler_params=pltpu.CompilerParams(vmem_limit_bytes=16 * 1024 * 1024),
        cost_estimate=pl.CostEstimate(
            flops=2 * tokens * rows * cols,
            bytes_accessed=2 * rows * cols + 4 * tokens * cols,
            transcendentals=0),
    )(hidden, head_rows)


def stats_kernel(count, *refs):
    student_refs, target_ref, out_ref = refs[:count], refs[count], refs[count + 1]
    height = student_refs[0].shape[0]
    for i, student_ref in enumerate(student_refs):
        at = pl.ds(i * height, height)
        student = student_ref[...]
        target = target_ref[i].astype(jnp.float32)
        student_top = jnp.max(student, axis=1, keepdims=True)
        target_top = jnp.max(target, axis=1, keepdims=True)
        target_exp = jnp.exp(target - target_top)
        out_ref[at, 0:1] = student_top
        out_ref[at, 1:2] = target_top
        out_ref[at, 2:3] = jnp.sum(jnp.exp(student - student_top), axis=1, keepdims=True)
        out_ref[at, 3:4] = jnp.sum(target_exp, axis=1, keepdims=True)
        out_ref[at, 4:5] = jnp.sum(target_exp * (target - student), axis=1, keepdims=True)


def row_stats(students, targets):
    count = len(students)
    height, cols = students[0].shape
    stats = pl.pallas_call(
        functools.partial(stats_kernel, count),
        out_shape=jax.ShapeDtypeStruct((count * height, 5), jnp.float32),
        compiler_params=pltpu.CompilerParams(
            vmem_limit_bytes=(8 * count * height * cols + 16 * 1024 * 1024)),
        cost_estimate=pl.CostEstimate(
            flops=12 * count * height * cols,
            bytes_accessed=6 * count * height * cols,
            transcendentals=2 * count * height * cols),
    )(*students, targets)
    return stats.T


def body(hidden_states, head_weight, teacher_logits):
    seq_count = lax.axis_size("seq")
    vocab_count = lax.axis_size("vocab")
    half = seq_count // 2
    last = seq_count - 1
    z = lax.axis_index("seq")
    own_tokens, width = hidden_states.shape
    rows, cols = head_weight.shape
    per_dev = teacher_logits.shape[1]
    chunk = half * per_dev
    chunks = vocab_count
    total_tokens = own_tokens * seq_count
    hops = seq_count - 1
    low_side = z < half

    def hop(value, j):
        return lax.ppermute(value, "seq", [(last - j, last - j - 1), (j, j + 1)])

    strips = [
        lax.dynamic_slice_in_dim(hidden_states, ((z + k) % seq_count) * rows, rows, axis=1)
        for k in range(seq_count)
    ]
    blocks = [strips[0]] + [
        lax.ppermute(strips[k], "seq", [(d, (d + k) % seq_count) for d in range(seq_count)])
        for k in range(1, seq_count)
    ]
    blocks = jnp.stack(blocks).reshape(seq_count, vocab_count, per_dev, rows)
    sides = []
    for end in (jnp.where(low_side, 0, last), jnp.where(low_side, last, 0)):
        step = jnp.where(end == 0, 1, -1)
        sides.append(jnp.stack(
            [blocks[(z - (end + step * j)) % seq_count] for j in range(half)], axis=1))
    ordered = jnp.stack(sides).reshape(total_tokens, rows)
    head_rows = head_weight.T
    half_tokens = total_tokens // 2

    mine, ordered = lax.optimization_barrier((teacher_logits[0], ordered))
    held = [mine] + [
        lax.ppermute(mine, "seq", [(j, 0), (last - j, last)]) for j in range(1, half)
    ]

    loads = [[i, i + 1] for i in range(0, chunks - 3, 2)] + [[chunks - 2], [chunks - 1]]
    moving = [None] * chunks
    students = [None] * chunks
    targets = []
    locals_ = []
    exchanged = []
    travels = {}
    settled_loss = []
    tie = []

    def tied(value):
        value = after(value, *tie) if tie else value
        tie[:] = [value]
        return value

    def send(i, j):
        part = (other_part if j < half else own_part)[i]
        if j == 0:
            value = tied(part)
        else:
            value = part + tied(moving[i])
            tie[:] = [value]
        moving[i] = hop(value, j)

    def exchange_teacher():
        rows_held = tied(jnp.concatenate(held, axis=0))
        pieces = jnp.stack([rows_held[:, v * cols:(v + 1) * cols] for v in range(vocab_count)])
        tie[:] = [pieces]
        targets.append(
            lax.all_to_all(pieces, "vocab", split_axis=0, concat_axis=0, tiled=True))

    def hold_teacher():
        held[:] = lax.optimization_barrier((*held, *tie))[:half]
        tie[:] = [held[-1]]

    def hold_targets():
        targets[0] = tied(targets[0])

    def local_stats(first, stop):
        locals_.append(row_stats(
            [tied(students[first]), *students[first + 1:stop]], targets[0][first:stop]))
        tie[:] = [locals_[-1]]

    def exchange_stats():
        stats = jnp.concatenate(locals_, axis=1)
        stats = jnp.broadcast_to(stats, (vocab_count, *stats.shape))
        stats = lax.all_to_all(stats, "vocab", split_axis=0, concat_axis=0, tiled=True)
        student_max = jnp.max(stats[:, 0], axis=0)
        teacher_max = jnp.max(stats[:, 1], axis=0)
        student_scale = jnp.exp(stats[:, 0] - student_max)
        teacher_scale = jnp.exp(stats[:, 1] - teacher_max)
        student_sum = jnp.sum(stats[:, 2] * student_scale, axis=0)
        teacher_sum = jnp.sum(stats[:, 3] * teacher_scale, axis=0)
        cross = jnp.sum(stats[:, 4] * teacher_scale, axis=0)
        exchanged.extend(lax.optimization_barrier(
            (student_max, student_sum, teacher_max, teacher_sum, cross)))
        tie[:] = [exchanged[0]]

    def form_grads(p):
        student_max, student_sum, teacher_max, teacher_sum, _ = exchanged
        grads = []
        for i in loads[p]:
            at = slice(i * chunk, (i + 1) * chunk)
            student = tied(students[i])
            target = targets[0][i].astype(jnp.float32)
            grads.append((
                LOSS_SCALE * (
                    jnp.exp(student - student_max[at, None]) / student_sum[at, None]
                    - jnp.exp(target - teacher_max[at, None]) / teacher_sum[at, None]
                )
            ).astype(jnp.bfloat16))
        grad = jnp.concatenate(grads, axis=0)
        tie[:] = [grad]
        travels[p] = [grad]

    def send_grad(p, j):
        value = travels[p][j] if j == 0 else tied(travels[p][j])
        travels[p].append(hop(value, j))

    def sum_up(i):
        students[i] = own_part[i] + tied(moving[i])
        tie[:] = [students[i]]

    def loss():
        student_max, student_sum, teacher_max, teacher_sum, cross = exchanged
        divergence = jnp.sum(
            cross / teacher_sum
            - teacher_max
            - jnp.log(teacher_sum)
            + student_max
            + jnp.log(student_sum)
        )
        travels["loss"] = [tied(divergence.reshape(1, 1))]

    def send_loss(j):
        value = travels["loss"][j] if j == 0 else tied(travels["loss"][j])
        travels["loss"].append(hop(value, j))

    near = jnp.minimum(z, last - z)

    def settle(key):
        own, other = travels[key][0], travels[key][hops]
        for j in range(1, half):
            own = jnp.where(near == j, travels[key][j], own)
            other = jnp.where(near == j, travels[key][hops - j], other)
        return own, other

    def settled(keys):
        pairs = [settle(key) for key in keys]
        return jnp.concatenate([p[0] for p in pairs] + [p[1] for p in pairs], axis=0)

    features = []

    def settle_loss():
        travels["loss"][hops] = tied(travels["loss"][hops])
        settled_loss.append(sum(settle("loss"))[0, 0] / total_tokens)
        tie[:] = [settled_loss[0]]

    def early_feature():
        grads = tied(settled(early_keys))
        features.append((grads, jnp.dot(grads, head_rows, preferred_element_type=jnp.float32)))
        tie[:] = [features[0][1]]

    slots = {}

    def plan(slot, order, call, *args):
        slots.setdefault(slot, []).append((order, len(slots.get(slot, ())), call, args))

    for i in range(chunks):
        plan(i - 1, 5, send, i, 0)
        for j in range(1, hops):
            plan(i + j, j, send, i, j)
        plan(i + hops, 4, sum_up, i)
    end = chunks + hops - 1
    plan(2, 0, hold_teacher)
    plan(3, 15, exchange_teacher)
    plan(6, 0, hold_targets)
    plan(end - 1, 15, local_stats, 0, chunks - 2)
    plan(end, 15, local_stats, chunks - 2, chunks)
    plan(end, 16, exchange_stats)
    count = len(loads)
    early_keys, late_keys = list(range(count // 2)), list(range(count // 2, count))
    for p in range(count):
        step = min(p, count - 2)
        plan(end + max(step, 1), 40 + 2 * p, form_grads, p)
        plan(end + max(step, 1), 41 + 2 * p, send_grad, p, 0)
        for j in range(1, hops):
            plan(end + 1 + step + j, 30 - j, send_grad, p, j)
    plan(end + 1, 35, loss)
    for j in range(hops):
        plan(end + 1, 36 if j == 0 else 41 + 2 * min(j - 1, 1), send_loss, j)
    plan(end + 1, 50, settle_loss)
    final = max(slots)
    plan(final, 700, early_feature)

    first_part = jnp.dot(
        ordered[half_tokens:half_tokens + chunk], head_weight, preferred_element_type=jnp.float32)
    other_part = [first_part]
    own_part = None
    for slot in sorted(slots):
        for _, _, call, args in sorted(slots[slot], key=lambda e: e[:2]):
            call(*args)
        if own_part is None:
            remaining = tied(jnp.concatenate(
                [ordered[half_tokens + chunk:], ordered[:half_tokens]]))
            parts = partial_students(remaining, head_rows, chunk)
            other_part.extend(parts[:chunks - 1])
            own_part = parts[chunks - 1:]
            tie[:] = [own_part[0]]

    mean_divergence = settled_loss[0]
    early_grads, feature_early = features[0]
    for key in late_keys:
        travels[key][hops] = tied(travels[key][hops])
    late_grads = settled(late_keys)
    feature_late = jnp.dot(late_grads, head_rows, preferred_element_type=jnp.float32)
    early_rows = early_grads.shape[0] // 2
    feature = jnp.concatenate(
        [feature_early.reshape(2, -1, rows), feature_late.reshape(2, -1, rows)], axis=1)
    both = ordered.reshape(2, half_tokens, rows)
    matching = jnp.concatenate([
        both[:, :early_rows].reshape(-1, rows), both[:, early_rows:].reshape(-1, rows)])
    all_grads = jnp.concatenate([early_grads, late_grads])
    head_part = lax.dot_general(
        all_grads, matching, (((0,), (0,)), ((), ())), preferred_element_type=jnp.float32
    ).T
    feature = feature.reshape(2, vocab_count, half, per_dev, rows).transpose(0, 2, 1, 3, 4)
    feature = feature.reshape(2, half, own_tokens, rows)
    low = jnp.where(low_side, feature[0], feature[1])
    high = jnp.where(low_side, feature[1], feature[0])
    feature = jnp.concatenate([low, high[::-1]])
    if vocab_count % seq_count == 0:
        share = vocab_count // seq_count
        out_cols = rows // share
        feature = feature.reshape(seq_count, own_tokens, share, out_cols).transpose(0, 2, 1, 3)
        feature = feature.reshape(vocab_count, own_tokens, out_cols)
        feature = lax.all_to_all(feature, "vocab", split_axis=0, concat_axis=0, tiled=True)
        feature, head_part = lax.optimization_barrier((feature, head_part))
        feature = jnp.sum(feature, axis=0)
        pairs = [
            ((dst * share + b) * seq_count + src, (src * share + b) * seq_count + dst)
            for src in range(seq_count) for dst in range(seq_count) for b in range(share)
        ]
        hidden_grad = lax.ppermute(feature, ("vocab", "seq"), pairs)
    else:
        feature = lax.all_to_all(feature, "seq", split_axis=0, concat_axis=2, tiled=True)
        hidden_grad = lax.psum_scatter(feature[0], "vocab", scatter_dimension=1, tiled=True)
    return (mean_divergence, hidden_grad, head_part)


def solution(mesh):
    in_specs = (P("seq", None), P("seq", "vocab"), P("seq", "vocab", None))
    out_specs = (P(), P("seq", "vocab"), P("seq", "vocab"))
    return jax.shard_map(body, mesh=mesh, in_specs=in_specs, out_specs=out_specs, check_vma=False)
```

```python
import functools

import jax
import jax.numpy as jnp
from jax import lax
from jax.experimental import pallas as pl
from jax.experimental.pallas import tpu as pltpu
from jax.sharding import PartitionSpec as P

LOSS_SCALE = 256.0
VOCAB_TILE = 1024


def after(value, *others):
    return lax.optimization_barrier((value, *others))[0]


def partial_kernel(hidden_ref, head_ref, *out_refs):
    product = lax.dot_general(
        hidden_ref[...], head_ref[...], (((1,), (1,)), ((), ())),
        preferred_element_type=jnp.float32)
    height = out_refs[0].shape[0]
    for i, out_ref in enumerate(out_refs):
        out_ref[...] = product[i * height:(i + 1) * height]


def partial_students(hidden, head_rows, chunk):
    tokens, rows = hidden.shape
    cols = head_rows.shape[0]
    tile = min(VOCAB_TILE, cols)
    count = tokens // chunk
    return pl.pallas_call(
        partial_kernel,
        grid=(pl.cdiv(cols, tile),),
        in_specs=[
            pl.BlockSpec((tokens, rows), lambda i: (0, 0)),
            pl.BlockSpec((tile, rows), lambda i: (i, 0)),
        ],
        out_specs=[pl.BlockSpec((chunk, tile), lambda i: (0, i))] * count,
        out_shape=[jax.ShapeDtypeStruct((chunk, cols), jnp.float32)] * count,
        compiler_params=pltpu.CompilerParams(vmem_limit_bytes=16 * 1024 * 1024),
        cost_estimate=pl.CostEstimate(
            flops=2 * tokens * rows * cols,
            bytes_accessed=2 * rows * cols + 4 * tokens * cols,
            transcendentals=0),
    )(hidden, head_rows)


def stats_kernel(count, *refs):
    student_refs, target_ref, out_ref = refs[:count], refs[count], refs[count + 1]
    height = student_refs[0].shape[0]
    for i, student_ref in enumerate(student_refs):
        at = pl.ds(i * height, height)
        student = student_ref[...]
        target = target_ref[i].astype(jnp.float32)
        student_top = jnp.max(student, axis=1, keepdims=True)
        target_top = jnp.max(target, axis=1, keepdims=True)
        target_exp = jnp.exp(target - target_top)
        out_ref[at, 0:1] = student_top
        out_ref[at, 1:2] = target_top
        out_ref[at, 2:3] = jnp.sum(jnp.exp(student - student_top), axis=1, keepdims=True)
        out_ref[at, 3:4] = jnp.sum(target_exp, axis=1, keepdims=True)
        out_ref[at, 4:5] = jnp.sum(target_exp * (target - student), axis=1, keepdims=True)


def row_stats(students, targets):
    count = len(students)
    height, cols = students[0].shape
    stats = pl.pallas_call(
        functools.partial(stats_kernel, count),
        out_shape=jax.ShapeDtypeStruct((count * height, 5), jnp.float32),
        compiler_params=pltpu.CompilerParams(
            vmem_limit_bytes=(8 * count * height * cols + 16 * 1024 * 1024)),
        cost_estimate=pl.CostEstimate(
            flops=12 * count * height * cols,
            bytes_accessed=6 * count * height * cols,
            transcendentals=2 * count * height * cols),
    )(*students, targets)
    return stats.T


def head_kernel(grad_ref, hidden_ref, *refs):
    out_ref = refs[-1]
    out_ref[...] = lax.dot_general(
        grad_ref[...], hidden_ref[...], (((0,), (0,)), ((), ())),
        preferred_element_type=jnp.float32)


def head_product(grads, hidden, first, stop, tile, out=None):
    tokens, cols = grads.shape
    rows = hidden.shape[1]
    return pl.pallas_call(
        head_kernel,
        grid=(stop - first,),
        in_specs=[
            pl.BlockSpec((tokens, tile), lambda i: (0, first + i)),
            pl.BlockSpec((tokens, rows), lambda i: (0, 0)),
        ] + ([] if out is None else [pl.BlockSpec(memory_space=pl.ANY)]),
        out_specs=pl.BlockSpec((tile, rows), lambda i: (first + i, 0)),
        out_shape=jax.ShapeDtypeStruct((cols, rows), jnp.float32),
        input_output_aliases={} if out is None else {2: 0},
        compiler_params=pltpu.CompilerParams(vmem_limit_bytes=24 * 1024 * 1024),
        cost_estimate=pl.CostEstimate(
            flops=2 * tokens * rows * tile * (stop - first),
            bytes_accessed=(4 * rows + 2 * tokens) * tile * (stop - first),
            transcendentals=0),
    )(grads, hidden, *([] if out is None else [out]))


def body(hidden_states, head_weight, teacher_logits):
    seq_count = lax.axis_size("seq")
    vocab_count = lax.axis_size("vocab")
    half = seq_count // 2
    last = seq_count - 1
    z = lax.axis_index("seq")
    own_tokens, width = hidden_states.shape
    rows, cols = head_weight.shape
    per_dev = teacher_logits.shape[1]
    chunk = half * per_dev
    chunks = vocab_count
    total_tokens = own_tokens * seq_count
    hops = seq_count - 1
    low_side = z < half

    def hop(value, j):
        return lax.ppermute(value, "seq", [(last - j, last - j - 1), (j, j + 1)])

    strips = [
        lax.dynamic_slice_in_dim(hidden_states, ((z + k) % seq_count) * rows, rows, axis=1)
        for k in range(seq_count)
    ]
    blocks = [strips[0]] + [
        lax.ppermute(strips[k], "seq", [(d, (d + k) % seq_count) for d in range(seq_count)])
        for k in range(1, seq_count)
    ]
    blocks = jnp.stack(blocks).reshape(seq_count, vocab_count, per_dev, rows)
    sides = []
    for end in (jnp.where(low_side, 0, last), jnp.where(low_side, last, 0)):
        step = jnp.where(end == 0, 1, -1)
        sides.append(jnp.stack(
            [blocks[(z - (end + step * j)) % seq_count] for j in range(half)], axis=1))
    ordered = jnp.stack(sides).reshape(total_tokens, rows)
    head_rows = head_weight.T
    half_tokens = total_tokens // 2

    mine, ordered = lax.optimization_barrier((teacher_logits[0], ordered))
    held = [mine] + [
        lax.ppermute(mine, "seq", [(j, 0), (last - j, last)]) for j in range(1, half)
    ]

    loads = [[i, i + 1] for i in range(0, chunks - 3, 2)] + [[chunks - 2], [chunks - 1]]
    moving = [None] * chunks
    students = [None] * chunks
    targets = []
    locals_ = []
    exchanged = []
    travels = {}
    settled_loss = []
    tie = []

    def tied(value):
        value = after(value, *tie) if tie else value
        tie[:] = [value]
        return value

    def send(i, j):
        part = (other_part if j < half else own_part)[i]
        if j == 0:
            value = tied(part)
        else:
            value = part + tied(moving[i])
            tie[:] = [value]
        moving[i] = hop(value, j)

    def exchange_teacher():
        rows_held = tied(jnp.concatenate(held, axis=0))
        pieces = jnp.stack([rows_held[:, v * cols:(v + 1) * cols] for v in range(vocab_count)])
        tie[:] = [pieces]
        targets.append(
            lax.all_to_all(pieces, "vocab", split_axis=0, concat_axis=0, tiled=True))

    def hold_teacher():
        held[:] = lax.optimization_barrier((*held, *tie))[:half]
        tie[:] = [held[-1]]

    def hold_targets():
        targets[0] = tied(targets[0])

    def local_stats(first, stop):
        locals_.append(row_stats(
            [tied(students[first]), *students[first + 1:stop]], targets[0][first:stop]))
        tie[:] = [locals_[-1]]

    def exchange_stats():
        stats = jnp.concatenate(locals_, axis=1)
        stats = jnp.broadcast_to(stats, (vocab_count, *stats.shape))
        stats = lax.all_to_all(stats, "vocab", split_axis=0, concat_axis=0, tiled=True)
        student_max = jnp.max(stats[:, 0], axis=0)
        teacher_max = jnp.max(stats[:, 1], axis=0)
        student_scale = jnp.exp(stats[:, 0] - student_max)
        teacher_scale = jnp.exp(stats[:, 1] - teacher_max)
        student_sum = jnp.sum(stats[:, 2] * student_scale, axis=0)
        teacher_sum = jnp.sum(stats[:, 3] * teacher_scale, axis=0)
        cross = jnp.sum(stats[:, 4] * teacher_scale, axis=0)
        exchanged.extend(lax.optimization_barrier(
            (student_max, student_sum, teacher_max, teacher_sum, cross)))
        tie[:] = [exchanged[0]]

    def form_grads(p):
        student_max, student_sum, teacher_max, teacher_sum, _ = exchanged
        grads = []
        for i in loads[p]:
            at = slice(i * chunk, (i + 1) * chunk)
            student = tied(students[i])
            target = targets[0][i].astype(jnp.float32)
            grads.append((
                LOSS_SCALE * (
                    jnp.exp(student - student_max[at, None]) / student_sum[at, None]
                    - jnp.exp(target - teacher_max[at, None]) / teacher_sum[at, None]
                )
            ).astype(jnp.bfloat16))
        grad = jnp.concatenate(grads, axis=0)
        tie[:] = [grad]
        travels[p] = [grad]

    def send_grad(p, j):
        value = travels[p][j] if j == 0 else tied(travels[p][j])
        travels[p].append(hop(value, j))

    def sum_up(i):
        students[i] = own_part[i] + tied(moving[i])
        tie[:] = [students[i]]

    def loss():
        student_max, student_sum, teacher_max, teacher_sum, cross = exchanged
        divergence = jnp.sum(
            cross / teacher_sum
            - teacher_max
            - jnp.log(teacher_sum)
            + student_max
            + jnp.log(student_sum)
        )
        travels["loss"] = [tied(divergence.reshape(1, 1))]

    def send_loss(j):
        value = travels["loss"][j] if j == 0 else tied(travels["loss"][j])
        travels["loss"].append(hop(value, j))

    near = jnp.minimum(z, last - z)

    def settle(key):
        own, other = travels[key][0], travels[key][hops]
        for j in range(1, half):
            own = jnp.where(near == j, travels[key][j], own)
            other = jnp.where(near == j, travels[key][hops - j], other)
        return own, other

    def settled(keys):
        pairs = [settle(key) for key in keys]
        return jnp.concatenate([p[0] for p in pairs] + [p[1] for p in pairs], axis=0)

    features = []

    def settle_loss():
        travels["loss"][hops] = tied(travels["loss"][hops])
        settled_loss.append(sum(settle("loss"))[0, 0] / total_tokens)
        tie[:] = [settled_loss[0]]

    def early_feature():
        grads = tied(settled(early_keys))
        features.append((grads, jnp.dot(grads, head_rows, preferred_element_type=jnp.float32)))
        tie[:] = [features[0][1]]

    slots = {}

    def plan(slot, order, call, *args):
        slots.setdefault(slot, []).append((order, len(slots.get(slot, ())), call, args))

    for i in range(chunks):
        plan(i - 1, 5, send, i, 0)
        for j in range(1, hops):
            plan(i + j, j, send, i, j)
        plan(i + hops, 4, sum_up, i)
    end = chunks + hops - 1
    plan(2, 0, hold_teacher)
    plan(3, 15, exchange_teacher)
    plan(6, 0, hold_targets)
    plan(end - 1, 15, local_stats, 0, chunks - 2)
    plan(end, 15, local_stats, chunks - 2, chunks)
    plan(end, 16, exchange_stats)
    count = len(loads)
    early_keys, late_keys = list(range(count // 2)), list(range(count // 2, count))
    for p in range(count):
        step = min(p, count - 2)
        plan(end + 1, 40 + 4 * p, form_grads, p)
        plan(end + 1, 41 + 4 * p, send_grad, p, 0)
        for j in range(1, hops):
            plan(end + 1 + step + j, 30 + j, send_grad, p, j)
    plan(end + 1, 35, loss)
    for j in range(hops):
        plan(end + 1, 36 if j == 0 else 42 + 4 * min(j - 1, 1), send_loss, j)
    plan(end + 3, 90, settle_loss)
    final = max(slots)
    plan(final, 700, early_feature)

    first_part = jnp.dot(
        ordered[half_tokens:half_tokens + chunk], head_weight, preferred_element_type=jnp.float32)
    other_part = [first_part]
    own_part = None
    for slot in sorted(slots):
        for _, _, call, args in sorted(slots[slot], key=lambda e: e[:2]):
            call(*args)
        if own_part is None:
            remaining = tied(jnp.concatenate(
                [ordered[half_tokens + chunk:], ordered[:half_tokens]]))
            parts = partial_students(remaining, head_rows, chunk)
            other_part.extend(parts[:chunks - 1])
            own_part = parts[chunks - 1:]
            tie[:] = [own_part[0]]

    mean_divergence = settled_loss[0]
    early_grads, feature_early = features[0]
    for key in late_keys:
        travels[key][hops] = tied(travels[key][hops])
    late_grads = settled(late_keys)
    feature_late = jnp.dot(late_grads, head_rows, preferred_element_type=jnp.float32)
    early_rows = early_grads.shape[0] // 2
    feature = jnp.concatenate(
        [feature_early.reshape(2, -1, rows), feature_late.reshape(2, -1, rows)], axis=1)
    both = ordered.reshape(2, half_tokens, rows)
    matching = jnp.concatenate([
        both[:, :early_rows].reshape(-1, rows), both[:, early_rows:].reshape(-1, rows)])
    all_grads = jnp.concatenate([early_grads, late_grads])
    tile = min(VOCAB_TILE, cols)
    blocks_out = pl.cdiv(cols, tile)
    beside = (blocks_out * 3 + 4) // 5
    feature = feature.reshape(2, vocab_count, half, per_dev, rows).transpose(0, 2, 1, 3, 4)
    feature = feature.reshape(2, half, own_tokens, rows)
    low = jnp.where(low_side, feature[0], feature[1])
    high = jnp.where(low_side, feature[1], feature[0])
    feature = jnp.concatenate([low, high[::-1]])
    if vocab_count % seq_count == 0:
        share = vocab_count // seq_count
        out_cols = rows // share
        feature = feature.reshape(seq_count, own_tokens, share, out_cols).transpose(0, 2, 1, 3)
        feature = feature.reshape(vocab_count, own_tokens, out_cols)
        feature = lax.all_to_all(feature, "vocab", split_axis=0, concat_axis=0, tiled=True)
        head_part = head_product(all_grads, matching, 0, beside, tile)
        feature, head_part = lax.optimization_barrier((feature, head_part))
        feature = jnp.sum(feature, axis=0)
        feature, head_part = lax.optimization_barrier((feature, head_part))
        pairs = [
            ((dst * share + b) * seq_count + src, (src * share + b) * seq_count + dst)
            for src in range(seq_count) for dst in range(seq_count) for b in range(share)
        ]
        hidden_grad = lax.ppermute(feature, ("vocab", "seq"), pairs)
        if beside < blocks_out:
            head_part = head_product(all_grads, matching, beside, blocks_out, tile, head_part)
    else:
        feature = lax.all_to_all(feature, "seq", split_axis=0, concat_axis=2, tiled=True)
        hidden_grad = lax.psum_scatter(feature[0], "vocab", scatter_dimension=1, tiled=True)
        head_part = head_product(all_grads, matching, 0, blocks_out, tile)
    return (mean_divergence, hidden_grad, head_part.T)


def solution(mesh):
    in_specs = (P("seq", None), P("seq", "vocab"), P("seq", "vocab", None))
    out_specs = (P(), P("seq", "vocab"), P("seq", "vocab"))
    return jax.shard_map(body, mesh=mesh, in_specs=in_specs, out_specs=out_specs, check_vma=False)
```

```python
import functools

import jax
import jax.numpy as jnp
from jax import lax
from jax.experimental import pallas as pl
from jax.experimental.pallas import tpu as pltpu
from jax.sharding import PartitionSpec as P

LOSS_SCALE = 256.0
VOCAB_TILE = 1024
STREAMS = 4


def after(value, *others):
    return lax.optimization_barrier((value, *others))[0]


def partial_kernel(hidden_ref, *refs):
    head_refs, out_refs = refs[:STREAMS], refs[STREAMS:]
    height = out_refs[0].shape[0]
    width = head_refs[0].shape[0]
    for k, head_ref in enumerate(head_refs):
        product = lax.dot_general(
            hidden_ref[...], head_ref[...], (((1,), (1,)), ((), ())),
            preferred_element_type=jnp.float32)
        for i, out_ref in enumerate(out_refs):
            out_ref[:, k * width:(k + 1) * width] = product[i * height:(i + 1) * height]


def partial_students(hidden, head_rows, chunk):
    tokens, rows = hidden.shape
    cols = head_rows.shape[0]
    width = VOCAB_TILE // STREAMS
    most = pl.cdiv(cols, width) - 1
    count = tokens // chunk

    def stream(k):
        return pl.BlockSpec((width, rows), lambda i: (jnp.minimum(i * STREAMS + k, most), 0))

    return pl.pallas_call(
        partial_kernel,
        grid=(pl.cdiv(cols, VOCAB_TILE),),
        in_specs=[pl.BlockSpec((tokens, rows), lambda i: (0, 0))]
        + [stream(k) for k in range(STREAMS)],
        out_specs=[pl.BlockSpec((chunk, VOCAB_TILE), lambda i: (0, i))] * count,
        out_shape=[jax.ShapeDtypeStruct((chunk, cols), jnp.float32)] * count,
        compiler_params=pltpu.CompilerParams(vmem_limit_bytes=16 * 1024 * 1024),
        cost_estimate=pl.CostEstimate(
            flops=2 * tokens * rows * cols,
            bytes_accessed=2 * rows * cols + 4 * tokens * cols,
            transcendentals=0),
    )(hidden, *[head_rows] * STREAMS)


def stats_kernel(count, *refs):
    student_refs, target_ref, out_ref = refs[:count], refs[count], refs[count + 1]
    height = student_refs[0].shape[0]
    for i, student_ref in enumerate(student_refs):
        at = pl.ds(i * height, height)
        student = student_ref[...]
        target = target_ref[i].astype(jnp.float32)
        student_top = jnp.max(student, axis=1, keepdims=True)
        target_top = jnp.max(target, axis=1, keepdims=True)
        target_exp = jnp.exp(target - target_top)
        out_ref[at, 0:1] = student_top
        out_ref[at, 1:2] = target_top
        out_ref[at, 2:3] = jnp.sum(jnp.exp(student - student_top), axis=1, keepdims=True)
        out_ref[at, 3:4] = jnp.sum(target_exp, axis=1, keepdims=True)
        out_ref[at, 4:5] = jnp.sum(target_exp * (target - student), axis=1, keepdims=True)


def row_stats(students, targets):
    count = len(students)
    height, cols = students[0].shape
    stats = pl.pallas_call(
        functools.partial(stats_kernel, count),
        out_shape=jax.ShapeDtypeStruct((count * height, 5), jnp.float32),
        compiler_params=pltpu.CompilerParams(
            vmem_limit_bytes=(8 * count * height * cols + 16 * 1024 * 1024)),
        cost_estimate=pl.CostEstimate(
            flops=12 * count * height * cols,
            bytes_accessed=6 * count * height * cols,
            transcendentals=2 * count * height * cols),
    )(*students, targets)
    return stats.T


def head_kernel(grad_ref, hidden_ref, *refs):
    out_ref = refs[-1]
    out_ref[...] = lax.dot_general(
        grad_ref[...], hidden_ref[...], (((0,), (0,)), ((), ())),
        preferred_element_type=jnp.float32)


def head_product(grads, hidden, first, stop, tile, out=None):
    tokens, cols = grads.shape
    rows = hidden.shape[1]
    return pl.pallas_call(
        head_kernel,
        grid=(stop - first,),
        in_specs=[
            pl.BlockSpec((tokens, tile), lambda i: (0, first + i)),
            pl.BlockSpec((tokens, rows), lambda i: (0, 0)),
        ] + ([] if out is None else [pl.BlockSpec(memory_space=pl.ANY)]),
        out_specs=pl.BlockSpec((tile, rows), lambda i: (first + i, 0)),
        out_shape=jax.ShapeDtypeStruct((cols, rows), jnp.float32),
        input_output_aliases={} if out is None else {2: 0},
        compiler_params=pltpu.CompilerParams(vmem_limit_bytes=56 * 1024 * 1024),
        cost_estimate=pl.CostEstimate(
            flops=2 * tokens * rows * tile * (stop - first),
            bytes_accessed=(4 * rows + 2 * tokens) * tile * (stop - first),
            transcendentals=0),
    )(grads, hidden, *([] if out is None else [out]))


def body(hidden_states, head_weight, teacher_logits):
    seq_count = lax.axis_size("seq")
    vocab_count = lax.axis_size("vocab")
    half = seq_count // 2
    last = seq_count - 1
    z = lax.axis_index("seq")
    own_tokens, width = hidden_states.shape
    rows, cols = head_weight.shape
    per_dev = teacher_logits.shape[1]
    chunk = half * per_dev
    chunks = vocab_count
    total_tokens = own_tokens * seq_count
    hops = seq_count - 1
    low_side = z < half

    def hop(value, j):
        return lax.ppermute(value, "seq", [(last - j, last - j - 1), (j, j + 1)])

    strips = [
        lax.dynamic_slice_in_dim(hidden_states, ((z + k) % seq_count) * rows, rows, axis=1)
        for k in range(seq_count)
    ]
    blocks = [strips[0]] + [
        lax.ppermute(strips[k], "seq", [(d, (d + k) % seq_count) for d in range(seq_count)])
        for k in range(1, seq_count)
    ]
    blocks = jnp.stack(blocks).reshape(seq_count, vocab_count, per_dev, rows)
    sides = []
    for end in (jnp.where(low_side, 0, last), jnp.where(low_side, last, 0)):
        step = jnp.where(end == 0, 1, -1)
        sides.append(jnp.stack(
            [blocks[(z - (end + step * j)) % seq_count] for j in range(half)], axis=1))
    ordered = jnp.stack(sides).reshape(total_tokens, rows)
    head_rows = head_weight.T
    half_tokens = total_tokens // 2

    mine, ordered = lax.optimization_barrier((teacher_logits[0], ordered))
    held = [mine] + [
        lax.ppermute(mine, "seq", [(j, 0), (last - j, last)]) for j in range(1, half)
    ]

    loads = [[i, i + 1] for i in range(0, chunks - 3, 2)] + [[chunks - 2], [chunks - 1]]
    moving = [None] * chunks
    students = [None] * chunks
    targets = []
    locals_ = []
    exchanged = []
    travels = {}
    settled_loss = []
    tie = []

    def tied(value):
        value = after(value, *tie) if tie else value
        tie[:] = [value]
        return value

    def send(i, j):
        part = (other_part if j < half else own_part)[i]
        if j == 0:
            value = tied(part)
        else:
            value = part + tied(moving[i])
            tie[:] = [value]
        moving[i] = hop(value, j)

    def exchange_teacher():
        rows_held = tied(jnp.concatenate(held, axis=0))
        pieces = jnp.stack([rows_held[:, v * cols:(v + 1) * cols] for v in range(vocab_count)])
        tie[:] = [pieces]
        targets.append(
            lax.all_to_all(pieces, "vocab", split_axis=0, concat_axis=0, tiled=True))

    def hold_teacher():
        held[:] = lax.optimization_barrier((*held, *tie))[:half]
        tie[:] = [held[-1]]

    def hold_targets():
        targets[0] = tied(targets[0])

    def local_stats(first, stop):
        locals_.append(row_stats(
            [tied(students[first]), *students[first + 1:stop]], targets[0][first:stop]))
        tie[:] = [locals_[-1]]

    def exchange_stats():
        stats = jnp.concatenate(locals_, axis=1)
        stats = jnp.broadcast_to(stats, (vocab_count, *stats.shape))
        stats = lax.all_to_all(stats, "vocab", split_axis=0, concat_axis=0, tiled=True)
        student_max = jnp.max(stats[:, 0], axis=0)
        teacher_max = jnp.max(stats[:, 1], axis=0)
        student_scale = jnp.exp(stats[:, 0] - student_max)
        teacher_scale = jnp.exp(stats[:, 1] - teacher_max)
        student_sum = jnp.sum(stats[:, 2] * student_scale, axis=0)
        teacher_sum = jnp.sum(stats[:, 3] * teacher_scale, axis=0)
        cross = jnp.sum(stats[:, 4] * teacher_scale, axis=0)
        exchanged.extend(lax.optimization_barrier(
            (student_max, student_sum, teacher_max, teacher_sum, cross)))
        tie[:] = [exchanged[0]]

    def form_grads(p):
        student_max, student_sum, teacher_max, teacher_sum, _ = exchanged
        grads = []
        for i in loads[p]:
            at = slice(i * chunk, (i + 1) * chunk)
            student = tied(students[i])
            target = targets[0][i].astype(jnp.float32)
            grads.append((
                LOSS_SCALE * (
                    jnp.exp(student - student_max[at, None]) / student_sum[at, None]
                    - jnp.exp(target - teacher_max[at, None]) / teacher_sum[at, None]
                )
            ).astype(jnp.bfloat16))
        grad = jnp.concatenate(grads, axis=0)
        tie[:] = [grad]
        travels[p] = [grad]

    def send_grad(p, j):
        value = travels[p][j] if j == 0 else tied(travels[p][j])
        travels[p].append(hop(value, j))

    def sum_up(i):
        students[i] = own_part[i] + tied(moving[i])
        tie[:] = [students[i]]

    def loss():
        student_max, student_sum, teacher_max, teacher_sum, cross = exchanged
        divergence = jnp.sum(
            cross / teacher_sum
            - teacher_max
            - jnp.log(teacher_sum)
            + student_max
            + jnp.log(student_sum)
        )
        travels["loss"] = [tied(divergence.reshape(1, 1))]

    def send_loss(j):
        value = travels["loss"][j] if j == 0 else tied(travels["loss"][j])
        travels["loss"].append(hop(value, j))

    near = jnp.minimum(z, last - z)

    def settle(key):
        own, other = travels[key][0], travels[key][hops]
        for j in range(1, half):
            own = jnp.where(near == j, travels[key][j], own)
            other = jnp.where(near == j, travels[key][hops - j], other)
        return own, other

    def settled(keys):
        pairs = [settle(key) for key in keys]
        return jnp.concatenate([p[0] for p in pairs] + [p[1] for p in pairs], axis=0)

    features = []
    early_settled = []

    def settle_loss():
        travels["loss"][hops] = tied(travels["loss"][hops])
        settled_loss.append(sum(settle("loss"))[0, 0] / total_tokens)
        tie[:] = [settled_loss[0]]

    def settle_early(p):
        travels[p][hops] = tied(travels[p][hops])
        early_settled.append(settle(p))
        tie[:] = [early_settled[-1][1]]

    def early_feature():
        grads = tied(jnp.concatenate([e[0] for e in early_settled] + [e[1] for e in early_settled]))
        features.append((grads, jnp.dot(grads, head_rows, preferred_element_type=jnp.float32)))
        tie[:] = [features[0][1]]

    slots = {}

    def plan(slot, order, call, *args):
        slots.setdefault(slot, []).append((order, len(slots.get(slot, ())), call, args))

    for i in range(chunks):
        plan(i - 1, 5, send, i, 0)
        for j in range(1, hops):
            plan(i + j, j, send, i, j)
        plan(i + hops, 4, sum_up, i)
    end = chunks + hops - 1
    plan(2, 0, hold_teacher)
    plan(3, 15, exchange_teacher)
    plan(6, 0, hold_targets)
    plan(end - 1, 15, local_stats, 0, chunks - 2)
    plan(end, 15, local_stats, chunks - 2, chunks)
    plan(end, 16, exchange_stats)
    count = len(loads)
    early_keys, late_keys = list(range(count // 2)), list(range(count // 2, count))
    for p in range(count):
        step = min(p, count - 2)
        plan(end + max(step, 1), 40 + 4 * p, form_grads, p)
        plan(end + max(step, 1), 41 + 4 * p, send_grad, p, 0)
        for j in range(1, hops):
            plan(end + 1 + step + j, 30 + 2 * j, send_grad, p, j)
        if p in early_keys:
            plan(end + 1 + step + hops, 33, settle_early, p)
    plan(end + 1, 35, loss)
    for j in range(hops):
        plan(end + 1, 36 if j == 0 else 42 + 4 * min(j - 1, 1), send_loss, j)
    plan(end + 3, 90, settle_loss)
    final = max(slots)
    plan(final, 700, early_feature)

    other_part = list(partial_students(
        ordered[half_tokens:half_tokens + chunk], head_rows, chunk))
    own_part = None
    for slot in sorted(slots):
        for _, _, call, args in sorted(slots[slot], key=lambda e: e[:2]):
            call(*args)
        if own_part is None:
            remaining = tied(jnp.concatenate(
                [ordered[half_tokens + chunk:], ordered[:half_tokens]]))
            parts = partial_students(remaining, head_rows, chunk)
            other_part.extend(parts[:chunks - 1])
            own_part = parts[chunks - 1:]
            tie[:] = [own_part[0]]

    mean_divergence = settled_loss[0]
    early_grads, feature_early = features[0]
    for key in late_keys:
        travels[key][hops] = tied(travels[key][hops])
    late_grads = settled(late_keys)
    feature_late = jnp.dot(late_grads, head_rows, preferred_element_type=jnp.float32)
    early_rows = early_grads.shape[0] // 2
    feature = jnp.concatenate(
        [feature_early.reshape(2, -1, rows), feature_late.reshape(2, -1, rows)], axis=1)
    both = ordered.reshape(2, half_tokens, rows)
    matching = jnp.concatenate([
        both[:, :early_rows].reshape(-1, rows), both[:, early_rows:].reshape(-1, rows)])
    all_grads = jnp.concatenate([early_grads, late_grads])
    tile = min(VOCAB_TILE, cols)
    blocks_out = pl.cdiv(cols, tile)
    beside = (blocks_out * 3 + 4) // 5
    feature = feature.reshape(2, vocab_count, half, per_dev, rows).transpose(0, 2, 1, 3, 4)
    feature = feature.reshape(2, half, own_tokens, rows)
    low = jnp.where(low_side, feature[0], feature[1])
    high = jnp.where(low_side, feature[1], feature[0])
    feature = jnp.concatenate([low, high[::-1]])
    if vocab_count % seq_count == 0:
        share = vocab_count // seq_count
        out_cols = rows // share
        feature = feature.reshape(seq_count, own_tokens, share, out_cols).transpose(0, 2, 1, 3)
        feature = feature.reshape(vocab_count, own_tokens, out_cols)
        feature = lax.all_to_all(feature, "vocab", split_axis=0, concat_axis=0, tiled=True)
        head_part = head_product(all_grads, matching, 0, beside, tile)
        feature, head_part = lax.optimization_barrier((feature, head_part))
        feature = jnp.sum(feature, axis=0)
        feature, head_part = lax.optimization_barrier((feature, head_part))
        pairs = [
            ((dst * share + b) * seq_count + src, (src * share + b) * seq_count + dst)
            for src in range(seq_count) for dst in range(seq_count) for b in range(share)
        ]
        hidden_grad = lax.ppermute(feature, ("vocab", "seq"), pairs)
        if beside < blocks_out:
            head_part = head_product(all_grads, matching, beside, blocks_out, tile, head_part)
    else:
        feature = lax.all_to_all(feature, "seq", split_axis=0, concat_axis=2, tiled=True)
        hidden_grad = lax.psum_scatter(feature[0], "vocab", scatter_dimension=1, tiled=True)
        head_part = head_product(all_grads, matching, 0, blocks_out, tile)
    return (mean_divergence, hidden_grad, head_part.T)


def solution(mesh):
    in_specs = (P("seq", None), P("seq", "vocab"), P("seq", "vocab", None))
    out_specs = (P(), P("seq", "vocab"), P("seq", "vocab"))
    return jax.shard_map(body, mesh=mesh, in_specs=in_specs, out_specs=out_specs, check_vma=False)
```

```python
import functools

import jax
import jax.numpy as jnp
from jax import lax
from jax.experimental import pallas as pl
from jax.experimental.pallas import tpu as pltpu
from jax.sharding import PartitionSpec as P

LOSS_SCALE = 256.0
VOCAB_TILE = 1024
STREAMS = 4


def after(value, *others):
    return lax.optimization_barrier((value, *others))[0]


def partial_kernel(hidden_ref, *refs):
    head_refs, out_refs = refs[:STREAMS], refs[STREAMS:]
    height = out_refs[0].shape[0]
    width = head_refs[0].shape[0]
    for k, head_ref in enumerate(head_refs):
        product = lax.dot_general(
            hidden_ref[...], head_ref[...], (((1,), (1,)), ((), ())),
            preferred_element_type=jnp.float32)
        for i, out_ref in enumerate(out_refs):
            out_ref[:, k * width:(k + 1) * width] = product[i * height:(i + 1) * height]


def partial_students(hidden, head_rows, chunk, grant):
    tokens, rows = hidden.shape
    cols = head_rows.shape[0]
    width = VOCAB_TILE // STREAMS
    most = pl.cdiv(cols, width) - 1
    count = tokens // chunk

    def stream(k):
        return pl.BlockSpec((width, rows), lambda i: (jnp.minimum(i * STREAMS + k, most), 0))

    return pl.pallas_call(
        partial_kernel,
        grid=(pl.cdiv(cols, VOCAB_TILE),),
        in_specs=[pl.BlockSpec((tokens, rows), lambda i: (0, 0))]
        + [stream(k) for k in range(STREAMS)],
        out_specs=[pl.BlockSpec((chunk, VOCAB_TILE), lambda i: (0, i))] * count,
        out_shape=[jax.ShapeDtypeStruct((chunk, cols), jnp.float32)] * count,
        compiler_params=pltpu.CompilerParams(vmem_limit_bytes=grant * 1024 * 1024),
        cost_estimate=pl.CostEstimate(
            flops=2 * tokens * rows * cols,
            bytes_accessed=2 * rows * cols + 4 * tokens * cols,
            transcendentals=0),
    )(hidden, *[head_rows] * STREAMS)


def stats_kernel(count, *refs):
    student_refs, target_ref, out_ref = refs[:count], refs[count], refs[count + 1]
    height = student_refs[0].shape[0]
    for i, student_ref in enumerate(student_refs):
        at = pl.ds(i * height, height)
        student = student_ref[...]
        target = target_ref[i].astype(jnp.float32)
        student_top = jnp.max(student, axis=1, keepdims=True)
        target_top = jnp.max(target, axis=1, keepdims=True)
        target_exp = jnp.exp(target - target_top)
        out_ref[at, 0:1] = student_top
        out_ref[at, 1:2] = target_top
        out_ref[at, 2:3] = jnp.sum(jnp.exp(student - student_top), axis=1, keepdims=True)
        out_ref[at, 3:4] = jnp.sum(target_exp, axis=1, keepdims=True)
        out_ref[at, 4:5] = jnp.sum(target_exp * (target - student), axis=1, keepdims=True)


def row_stats(students, targets):
    count = len(students)
    height, cols = students[0].shape
    stats = pl.pallas_call(
        functools.partial(stats_kernel, count),
        out_shape=jax.ShapeDtypeStruct((count * height, 5), jnp.float32),
        compiler_params=pltpu.CompilerParams(
            vmem_limit_bytes=(8 * count * height * cols + 16 * 1024 * 1024)),
        cost_estimate=pl.CostEstimate(
            flops=12 * count * height * cols,
            bytes_accessed=6 * count * height * cols,
            transcendentals=2 * count * height * cols),
    )(*students, targets)
    return stats.T


def head_kernel(grad_ref, hidden_ref, *refs):
    out_ref = refs[-1]
    out_ref[...] = lax.dot_general(
        grad_ref[...], hidden_ref[...], (((0,), (0,)), ((), ())),
        preferred_element_type=jnp.float32)


def head_product(grads, hidden, first, stop, tile, out=None):
    tokens, cols = grads.shape
    rows = hidden.shape[1]
    return pl.pallas_call(
        head_kernel,
        grid=(stop - first,),
        in_specs=[
            pl.BlockSpec((tokens, tile), lambda i: (0, first + i)),
            pl.BlockSpec((tokens, rows), lambda i: (0, 0)),
        ] + ([] if out is None else [pl.BlockSpec(memory_space=pl.ANY)]),
        out_specs=pl.BlockSpec((tile, rows), lambda i: (first + i, 0)),
        out_shape=jax.ShapeDtypeStruct((cols, rows), jnp.float32),
        input_output_aliases={} if out is None else {2: 0},
        compiler_params=pltpu.CompilerParams(vmem_limit_bytes=56 * 1024 * 1024),
        cost_estimate=pl.CostEstimate(
            flops=2 * tokens * rows * tile * (stop - first),
            bytes_accessed=(4 * rows + 2 * tokens) * tile * (stop - first),
            transcendentals=0),
    )(grads, hidden, *([] if out is None else [out]))


def body(hidden_states, head_weight, teacher_logits):
    seq_count = lax.axis_size("seq")
    vocab_count = lax.axis_size("vocab")
    half = seq_count // 2
    last = seq_count - 1
    z = lax.axis_index("seq")
    own_tokens, width = hidden_states.shape
    rows, cols = head_weight.shape
    per_dev = teacher_logits.shape[1]
    chunk = half * per_dev
    chunks = vocab_count
    total_tokens = own_tokens * seq_count
    hops = seq_count - 1
    low_side = z < half

    def hop(value, j):
        return lax.ppermute(value, "seq", [(last - j, last - j - 1), (j, j + 1)])

    strips = [
        lax.dynamic_slice_in_dim(hidden_states, ((z + k) % seq_count) * rows, rows, axis=1)
        for k in range(seq_count)
    ]
    blocks = [strips[0]] + [
        lax.ppermute(strips[k], "seq", [(d, (d + k) % seq_count) for d in range(seq_count)])
        for k in range(1, seq_count)
    ]
    blocks = jnp.stack(blocks).reshape(seq_count, vocab_count, per_dev, rows)
    sides = []
    for end in (jnp.where(low_side, 0, last), jnp.where(low_side, last, 0)):
        step = jnp.where(end == 0, 1, -1)
        sides.append(jnp.stack(
            [blocks[(z - (end + step * j)) % seq_count] for j in range(half)], axis=1))
    ordered = jnp.stack(sides).reshape(total_tokens, rows)
    head_rows = head_weight.T
    half_tokens = total_tokens // 2

    mine, ordered = lax.optimization_barrier((teacher_logits[0], ordered))
    held = [mine] + [
        lax.ppermute(mine, "seq", [(j, 0), (last - j, last)]) for j in range(1, half)
    ]

    middle = chunks // 2
    groups = [range(middle), range(middle, chunks)]
    loads = [[i, i + 1] for i in range(0, chunks - 3, 2)] + [[chunks - 2], [chunks - 1]]
    early_keys = [p for p, members in enumerate(loads) if members[-1] < middle]
    late_keys = [p for p in range(len(loads)) if p not in early_keys]
    moving = [None] * chunks
    students = [None] * chunks
    targets = []
    pieces = []
    locals_ = {0: [], 1: []}
    exchanged = {}
    travels = {}
    settled_loss = []
    tie = []

    def tied(value):
        value = after(value, *tie) if tie else value
        tie[:] = [value]
        return value

    def send(i, j):
        part = (other_part if j < half else own_part)[i]
        if j == 0:
            value = tied(part)
        else:
            value = part + tied(moving[i])
            tie[:] = [value]
        moving[i] = hop(value, j)

    def cut_teacher():
        rows_held = tied(jnp.concatenate(held, axis=0))
        pieces.append(jnp.stack(
            [rows_held[:, v * cols:(v + 1) * cols] for v in range(vocab_count)]))
        tie[:] = pieces

    def exchange_teacher():
        targets.append(
            lax.all_to_all(tied(pieces[0]), "vocab", split_axis=0, concat_axis=0, tiled=True))

    def hold_teacher():
        held[:] = lax.optimization_barrier((*held, *tie))[:half]
        tie[:] = [held[-1]]

    def hold_targets():
        targets[0] = tied(targets[0])

    def local_stats(g, first, stop):
        locals_[g].append(row_stats(
            [tied(students[first]), *students[first + 1:stop]], targets[0][first:stop]))
        tie[:] = [locals_[g][-1]]

    def exchange_stats(g):
        stats = jnp.concatenate(locals_[g], axis=1)
        stats = jnp.broadcast_to(stats, (vocab_count, *stats.shape))
        exchanged[g] = lax.all_to_all(stats, "vocab", split_axis=0, concat_axis=0, tiled=True)

    def merge_stats(g):
        stats = tied(exchanged[g])
        student_max = jnp.max(stats[:, 0], axis=0)
        teacher_max = jnp.max(stats[:, 1], axis=0)
        student_scale = jnp.exp(stats[:, 0] - student_max)
        teacher_scale = jnp.exp(stats[:, 1] - teacher_max)
        student_sum = jnp.sum(stats[:, 2] * student_scale, axis=0)
        teacher_sum = jnp.sum(stats[:, 3] * teacher_scale, axis=0)
        cross = jnp.sum(stats[:, 4] * teacher_scale, axis=0)
        exchanged[g] = lax.optimization_barrier(
            (student_max, student_sum, teacher_max, teacher_sum, cross))
        tie[:] = [exchanged[g][0]]

    def form_grads(p):
        g = 0 if p in early_keys else 1
        student_max, student_sum, teacher_max, teacher_sum, _ = exchanged[g]
        grads = []
        for i in loads[p]:
            at = slice((i - groups[g][0]) * chunk, (i - groups[g][0] + 1) * chunk)
            student = tied(students[i])
            target = targets[0][i].astype(jnp.float32)
            grads.append((
                LOSS_SCALE * (
                    jnp.exp(student - student_max[at, None]) / student_sum[at, None]
                    - jnp.exp(target - teacher_max[at, None]) / teacher_sum[at, None]
                )
            ).astype(jnp.bfloat16))
        grad = jnp.concatenate(grads, axis=0)
        tie[:] = [grad]
        travels[p] = [grad]

    def send_grad(p, j):
        value = travels[p][j] if j == 0 else tied(travels[p][j])
        travels[p].append(hop(value, j))

    def sum_up(i):
        students[i] = own_part[i] + tied(moving[i])
        tie[:] = [students[i]]

    def loss():
        student_max, student_sum, teacher_max, teacher_sum, cross = (
            jnp.concatenate(both) for both in zip(exchanged[0], exchanged[1]))
        divergence = jnp.sum(
            cross / teacher_sum
            - teacher_max
            - jnp.log(teacher_sum)
            + student_max
            + jnp.log(student_sum)
        )
        travels["loss"] = [tied(divergence.reshape(1, 1))]

    def send_loss(j):
        value = travels["loss"][j] if j == 0 else tied(travels["loss"][j])
        travels["loss"].append(hop(value, j))

    near = jnp.minimum(z, last - z)

    def settle(key):
        own, other = travels[key][0], travels[key][hops]
        for j in range(1, half):
            own = jnp.where(near == j, travels[key][j], own)
            other = jnp.where(near == j, travels[key][hops - j], other)
        return own, other

    def settled(keys):
        pairs = [settle(key) for key in keys]
        return jnp.concatenate([p[0] for p in pairs] + [p[1] for p in pairs], axis=0)

    features = []
    early_settled = []

    def settle_loss():
        travels["loss"][hops] = tied(travels["loss"][hops])
        settled_loss.append(sum(settle("loss"))[0, 0] / total_tokens)
        tie[:] = [settled_loss[0]]

    def settle_early(p):
        travels[p][hops] = tied(travels[p][hops])
        early_settled.append(settle(p))
        tie[:] = [early_settled[-1][1]]

    def early_feature():
        grads = tied(jnp.concatenate([e[0] for e in early_settled] + [e[1] for e in early_settled]))
        features.append((grads, jnp.dot(grads, head_rows, preferred_element_type=jnp.float32)))
        tie[:] = [features[0][1]]

    slots = {}

    def plan(slot, order, call, *args):
        slots.setdefault(slot, []).append((order, len(slots.get(slot, ())), call, args))

    for i in range(chunks):
        plan(i - 1, 5, send, i, 0)
        for j in range(1, hops):
            plan(i + j, j, send, i, j)
        plan(i + hops, 4, sum_up, i)
    end = chunks + hops - 1
    plan(2, 0, hold_teacher)
    plan(3, 15, cut_teacher)
    plan(3, 16, exchange_teacher)
    plan(6, 0, hold_targets)
    early_slot = middle + hops
    plan(early_slot, 15, local_stats, 0, 0, middle)
    plan(early_slot, 16, exchange_stats, 0)
    plan(early_slot + 1, 20, merge_stats, 0)
    for p in early_keys:
        plan(early_slot + 1 + p, 40, form_grads, p)
        plan(early_slot + 1 + p, 41, send_grad, p, 0)
        for j in range(1, hops):
            at = early_slot + 1 + p + j
            if at < end or p == 0:
                plan(at, (45 if at < end else 90) + j, send_grad, p, j)
            else:
                plan(at + 1, 60 + j, send_grad, p, j)
        plan(max(early_slot + 2 + p + hops, end + 2 + p) + (p > 0), 95, settle_early, p)
    if middle < chunks - 2:
        plan(end - 1, 15, local_stats, 1, middle, chunks - 2)
    plan(end, 15, local_stats, 1, chunks - 2, chunks)
    plan(end, 16, exchange_stats, 1)
    plan(end + 1, 20, merge_stats, 1)
    for p in late_keys:
        step = min(p - late_keys[0], len(late_keys) - 2)
        plan(end + 1, 40 + 2 * p, form_grads, p)
        plan(end + 1, 41 + 2 * p, send_grad, p, 0)
        for j in range(1, hops):
            plan(end + 1 + step + j, 30 + 2 * j, send_grad, p, j)
    plan(end + 1, 70, loss)
    for j in range(hops):
        plan(end + 1 + j + (j > 0), 98, send_loss, j)
    plan(end + 2 + hops, 99, settle_loss)
    final = max(slots)
    plan(final, 700, early_feature)

    other_part = list(partial_students(
        ordered[half_tokens:half_tokens + chunk], head_rows, chunk, 16))
    own_part = None
    for slot in sorted(slots):
        for _, _, call, args in sorted(slots[slot], key=lambda e: e[:2]):
            call(*args)
        if slot == -1:
            other_part.extend(partial_students(
                tied(ordered[half_tokens + chunk:]), head_rows, chunk, 16))
            tie[:] = [other_part[1]]
        if slot == 1:
            own_part = partial_students(tied(ordered[:half_tokens]), head_rows, chunk, 16)
            tie[:] = [own_part[0]]

    mean_divergence = settled_loss[0]
    early_grads, feature_early = features[0]
    for key in late_keys:
        travels[key][hops] = tied(travels[key][hops])
    late_grads = settled(late_keys)
    feature_late = jnp.dot(late_grads, head_rows, preferred_element_type=jnp.float32)
    early_rows = early_grads.shape[0] // 2
    feature = jnp.concatenate(
        [feature_early.reshape(2, -1, rows), feature_late.reshape(2, -1, rows)], axis=1)
    both = ordered.reshape(2, half_tokens, rows)
    matching = jnp.concatenate([
        both[:, :early_rows].reshape(-1, rows), both[:, early_rows:].reshape(-1, rows)])
    all_grads = jnp.concatenate([early_grads, late_grads])
    tile = min(VOCAB_TILE, cols)
    blocks_out = pl.cdiv(cols, tile)
    beside = (blocks_out * 3 + 4) // 5
    feature = feature.reshape(2, vocab_count, half, per_dev, rows).transpose(0, 2, 1, 3, 4)
    feature = feature.reshape(2, half, own_tokens, rows)
    low = jnp.where(low_side, feature[0], feature[1])
    high = jnp.where(low_side, feature[1], feature[0])
    feature = jnp.concatenate([low, high[::-1]])
    if vocab_count % seq_count == 0:
        share = vocab_count // seq_count
        out_cols = rows // share
        feature = feature.reshape(seq_count, own_tokens, share, out_cols).transpose(0, 2, 1, 3)
        feature = feature.reshape(vocab_count, own_tokens, out_cols)
        feature = lax.all_to_all(feature, "vocab", split_axis=0, concat_axis=0, tiled=True)
        head_part = head_product(all_grads, matching, 0, beside, tile)
        feature, head_part = lax.optimization_barrier((feature, head_part))
        feature = jnp.sum(feature, axis=0)
        feature, head_part = lax.optimization_barrier((feature, head_part))
        pairs = [
            ((dst * share + b) * seq_count + src, (src * share + b) * seq_count + dst)
            for src in range(seq_count) for dst in range(seq_count) for b in range(share)
        ]
        hidden_grad = lax.ppermute(feature, ("vocab", "seq"), pairs)
        if beside < blocks_out:
            head_part = head_product(all_grads, matching, beside, blocks_out, tile, head_part)
    else:
        feature = lax.all_to_all(feature, "seq", split_axis=0, concat_axis=2, tiled=True)
        hidden_grad = lax.psum_scatter(feature[0], "vocab", scatter_dimension=1, tiled=True)
        head_part = head_product(all_grads, matching, 0, blocks_out, tile)
    return (mean_divergence, hidden_grad, head_part.T)


def solution(mesh):
    in_specs = (P("seq", None), P("seq", "vocab"), P("seq", "vocab", None))
    out_specs = (P(), P("seq", "vocab"), P("seq", "vocab"))
    return jax.shard_map(body, mesh=mesh, in_specs=in_specs, out_specs=out_specs, check_vma=False)
```

```python
import functools

import jax
import jax.numpy as jnp
from jax import lax
from jax.experimental import pallas as pl
from jax.experimental.pallas import tpu as pltpu
from jax.sharding import PartitionSpec as P

LOSS_SCALE = 256.0
VOCAB_TILE = 1024
STREAMS = 4


def after(value, *others):
    return lax.optimization_barrier((value, *others))[0]


def partial_kernel(hidden_ref, *refs):
    head_refs, out_refs = refs[:STREAMS], refs[STREAMS:]
    height = out_refs[0].shape[0]
    width = head_refs[0].shape[0]
    for k, head_ref in enumerate(head_refs):
        product = lax.dot_general(
            hidden_ref[...], head_ref[...], (((1,), (1,)), ((), ())),
            preferred_element_type=jnp.float32)
        for i, out_ref in enumerate(out_refs):
            out_ref[:, k * width:(k + 1) * width] = product[i * height:(i + 1) * height]


def partial_students(hidden, head_rows, chunk, grant):
    tokens, rows = hidden.shape
    cols = head_rows.shape[0]
    width = VOCAB_TILE // STREAMS
    most = pl.cdiv(cols, width) - 1
    count = tokens // chunk

    def stream(k):
        return pl.BlockSpec((width, rows), lambda i: (jnp.minimum(i * STREAMS + k, most), 0))

    return pl.pallas_call(
        partial_kernel,
        grid=(pl.cdiv(cols, VOCAB_TILE),),
        in_specs=[pl.BlockSpec((tokens, rows), lambda i: (0, 0))]
        + [stream(k) for k in range(STREAMS)],
        out_specs=[pl.BlockSpec((chunk, VOCAB_TILE), lambda i: (0, i))] * count,
        out_shape=[jax.ShapeDtypeStruct((chunk, cols), jnp.float32)] * count,
        compiler_params=pltpu.CompilerParams(vmem_limit_bytes=grant * 1024 * 1024),
        cost_estimate=pl.CostEstimate(
            flops=2 * tokens * rows * cols,
            bytes_accessed=2 * rows * cols + 4 * tokens * cols,
            transcendentals=0),
    )(hidden, *[head_rows] * STREAMS)


def stats_kernel(count, *refs):
    student_refs, target_ref, out_ref = refs[:count], refs[count], refs[count + 1]
    height = student_refs[0].shape[0]
    for i, student_ref in enumerate(student_refs):
        at = pl.ds(i * height, height)
        student = student_ref[...]
        target = target_ref[i].astype(jnp.float32)
        student_top = jnp.max(student, axis=1, keepdims=True)
        target_top = jnp.max(target, axis=1, keepdims=True)
        target_exp = jnp.exp(target - target_top)
        out_ref[at, 0:1] = student_top
        out_ref[at, 1:2] = target_top
        out_ref[at, 2:3] = jnp.sum(jnp.exp(student - student_top), axis=1, keepdims=True)
        out_ref[at, 3:4] = jnp.sum(target_exp, axis=1, keepdims=True)
        out_ref[at, 4:5] = jnp.sum(target_exp * (target - student), axis=1, keepdims=True)


def row_stats(students, targets):
    count = len(students)
    height, cols = students[0].shape
    stats = pl.pallas_call(
        functools.partial(stats_kernel, count),
        out_shape=jax.ShapeDtypeStruct((count * height, 5), jnp.float32),
        compiler_params=pltpu.CompilerParams(
            vmem_limit_bytes=(8 * count * height * cols + 16 * 1024 * 1024)),
        cost_estimate=pl.CostEstimate(
            flops=12 * count * height * cols,
            bytes_accessed=6 * count * height * cols,
            transcendentals=2 * count * height * cols),
    )(*students, targets)
    return stats.T


def head_kernel(grad_ref, hidden_ref, *refs):
    out_ref = refs[-1]
    out_ref[...] = lax.dot_general(
        grad_ref[...], hidden_ref[...], (((0,), (0,)), ((), ())),
        preferred_element_type=jnp.float32)


def head_product(grads, hidden, first, stop, tile, out=None):
    tokens, cols = grads.shape
    rows = hidden.shape[1]
    return pl.pallas_call(
        head_kernel,
        grid=(stop - first,),
        in_specs=[
            pl.BlockSpec((tokens, tile), lambda i: (0, first + i)),
            pl.BlockSpec((tokens, rows), lambda i: (0, 0)),
        ] + ([] if out is None else [pl.BlockSpec(memory_space=pl.ANY)]),
        out_specs=pl.BlockSpec((tile, rows), lambda i: (first + i, 0)),
        out_shape=jax.ShapeDtypeStruct((cols, rows), jnp.float32),
        input_output_aliases={} if out is None else {2: 0},
        compiler_params=pltpu.CompilerParams(vmem_limit_bytes=56 * 1024 * 1024),
        cost_estimate=pl.CostEstimate(
            flops=2 * tokens * rows * tile * (stop - first),
            bytes_accessed=(4 * rows + 2 * tokens) * tile * (stop - first),
            transcendentals=0),
    )(grads, hidden, *([] if out is None else [out]))


def body(hidden_states, head_weight, teacher_logits):
    seq_count = lax.axis_size("seq")
    vocab_count = lax.axis_size("vocab")
    half = seq_count // 2
    last = seq_count - 1
    z = lax.axis_index("seq")
    own_tokens, width = hidden_states.shape
    rows, cols = head_weight.shape
    per_dev = teacher_logits.shape[1]
    chunk = half * per_dev
    chunks = vocab_count
    total_tokens = own_tokens * seq_count
    hops = seq_count - 1
    low_side = z < half

    def hop(value, j):
        return lax.ppermute(value, "seq", [(last - j, last - j - 1), (j, j + 1)])

    strips = [
        lax.dynamic_slice_in_dim(hidden_states, ((z + k) % seq_count) * rows, rows, axis=1)
        for k in range(seq_count)
    ]
    blocks = [strips[0]] + [
        lax.ppermute(strips[k], "seq", [(d, (d + k) % seq_count) for d in range(seq_count)])
        for k in range(1, seq_count)
    ]
    blocks = jnp.stack(blocks).reshape(seq_count, vocab_count, per_dev, rows)
    sides = []
    for end in (jnp.where(low_side, 0, last), jnp.where(low_side, last, 0)):
        step = jnp.where(end == 0, 1, -1)
        sides.append(jnp.stack(
            [blocks[(z - (end + step * j)) % seq_count] for j in range(half)], axis=1))
    ordered = jnp.stack(sides).reshape(total_tokens, rows)
    head_rows = head_weight.T
    half_tokens = total_tokens // 2

    mine, ordered = lax.optimization_barrier((teacher_logits[0], ordered))
    held = [mine] + [
        lax.ppermute(mine, "seq", [(j, 0), (last - j, last)]) for j in range(1, half)
    ]

    middle = chunks // 2
    groups = [range(middle), range(middle, chunks)]
    loads = [[i, i + 1] for i in range(0, chunks - 3, 2)] + [[chunks - 2], [chunks - 1]]
    early_keys = [p for p, members in enumerate(loads) if members[-1] < middle]
    late_keys = [p for p in range(len(loads)) if p not in early_keys]
    moving = [None] * chunks
    students = [None] * chunks
    targets = []
    pieces = []
    locals_ = {0: [], 1: []}
    exchanged = {}
    travels = {}
    settled_loss = []
    tie = []

    def tied(value):
        value = after(value, *tie) if tie else value
        tie[:] = [value]
        return value

    def send(i, j):
        part = (other_part if j < half else own_part)[i]
        if j == 0:
            value = tied(part)
        else:
            value = part + tied(moving[i])
            tie[:] = [value]
        moving[i] = hop(value, j)

    def cut_teacher():
        rows_held = tied(jnp.concatenate(held, axis=0))
        pieces.append(jnp.stack(
            [rows_held[:, v * cols:(v + 1) * cols] for v in range(vocab_count)]))
        tie[:] = pieces

    def exchange_teacher():
        targets.append(
            lax.all_to_all(tied(pieces[0]), "vocab", split_axis=0, concat_axis=0, tiled=True))

    def hold_teacher():
        held[:] = lax.optimization_barrier((*held, *tie))[:half]
        tie[:] = [held[-1]]

    def hold_targets():
        targets[0] = tied(targets[0])

    def local_stats(g, first, stop):
        locals_[g].append(row_stats(
            [tied(students[first]), *students[first + 1:stop]], targets[0][first:stop]))
        tie[:] = [locals_[g][-1]]

    def exchange_stats(g):
        stats = jnp.concatenate(locals_[g], axis=1)
        stats = jnp.broadcast_to(stats, (vocab_count, *stats.shape))
        exchanged[g] = lax.all_to_all(stats, "vocab", split_axis=0, concat_axis=0, tiled=True)

    def merge_stats(g):
        stats = tied(exchanged[g])
        student_max = jnp.max(stats[:, 0], axis=0)
        teacher_max = jnp.max(stats[:, 1], axis=0)
        student_scale = jnp.exp(stats[:, 0] - student_max)
        teacher_scale = jnp.exp(stats[:, 1] - teacher_max)
        student_sum = jnp.sum(stats[:, 2] * student_scale, axis=0)
        teacher_sum = jnp.sum(stats[:, 3] * teacher_scale, axis=0)
        cross = jnp.sum(stats[:, 4] * teacher_scale, axis=0)
        exchanged[g] = lax.optimization_barrier(
            (student_max, student_sum, teacher_max, teacher_sum, cross))
        tie[:] = [exchanged[g][0]]

    def form_grads(p):
        g = 0 if p in early_keys else 1
        student_max, student_sum, teacher_max, teacher_sum, _ = exchanged[g]
        grads = []
        for i in loads[p]:
            at = slice((i - groups[g][0]) * chunk, (i - groups[g][0] + 1) * chunk)
            student = tied(students[i])
            target = targets[0][i].astype(jnp.float32)
            grads.append((
                LOSS_SCALE * (
                    jnp.exp(student - student_max[at, None]) / student_sum[at, None]
                    - jnp.exp(target - teacher_max[at, None]) / teacher_sum[at, None]
                )
            ).astype(jnp.bfloat16))
        grad = jnp.concatenate(grads, axis=0)
        tie[:] = [grad]
        travels[p] = [grad]

    def send_grad(p, j):
        value = travels[p][j] if j == 0 else tied(travels[p][j])
        travels[p].append(hop(value, j))

    def sum_up(i):
        students[i] = own_part[i] + tied(moving[i])
        tie[:] = [students[i]]

    def loss():
        student_max, student_sum, teacher_max, teacher_sum, cross = (
            jnp.concatenate(both) for both in zip(exchanged[0], exchanged[1]))
        divergence = jnp.sum(
            cross / teacher_sum
            - teacher_max
            - jnp.log(teacher_sum)
            + student_max
            + jnp.log(student_sum)
        )
        travels["loss"] = [tied(divergence.reshape(1, 1))]

    def send_loss(j):
        value = travels["loss"][j] if j == 0 else tied(travels["loss"][j])
        travels["loss"].append(hop(value, j))

    near = jnp.minimum(z, last - z)

    def settle(key):
        own, other = travels[key][0], travels[key][hops]
        for j in range(1, half):
            own = jnp.where(near == j, travels[key][j], own)
            other = jnp.where(near == j, travels[key][hops - j], other)
        return own, other

    def settled(keys):
        pairs = [settle(key) for key in keys]
        return jnp.concatenate([p[0] for p in pairs] + [p[1] for p in pairs], axis=0)

    features = []
    early_settled = []

    def settle_loss():
        travels["loss"][hops] = tied(travels["loss"][hops])
        settled_loss.append(sum(settle("loss"))[0, 0] / total_tokens)
        tie[:] = [settled_loss[0]]

    def settle_early(p):
        travels[p][hops] = tied(travels[p][hops])
        early_settled.append(settle(p))
        tie[:] = [early_settled[-1][1]]

    def early_feature():
        grads = tied(jnp.concatenate([e[0] for e in early_settled] + [e[1] for e in early_settled]))
        features.append((grads, jnp.dot(grads, head_rows, preferred_element_type=jnp.float32)))
        tie[:] = [features[0][1]]

    slots = {}

    def plan(slot, order, call, *args):
        slots.setdefault(slot, []).append((order, len(slots.get(slot, ())), call, args))

    for i in range(chunks):
        plan(i - 1, 5, send, i, 0)
        for j in range(1, hops):
            plan(i + j, j, send, i, j)
        plan(i + hops, 4, sum_up, i)
    end = chunks + hops - 1
    plan(2, 0, hold_teacher)
    plan(3, 15, cut_teacher)
    plan(3, 16, exchange_teacher)
    plan(6, 0, hold_targets)
    early_slot = middle + hops
    plan(early_slot, 15, local_stats, 0, 0, middle)
    plan(early_slot, 16, exchange_stats, 0)
    plan(early_slot + 1, 20, merge_stats, 0)
    for p in early_keys:
        plan(early_slot + 1 + p, 40, form_grads, p)
        plan(early_slot + 1 + p, 41, send_grad, p, 0)
        for j in range(1, hops):
            at = early_slot + 1 + p + j
            if at < end or p == 0:
                plan(at, (45 if at < end else 90) + j, send_grad, p, j)
            else:
                plan(at + 1, 60 + j, send_grad, p, j)
        plan(max(early_slot + 2 + p + hops, end + 2 + p) + (p > 0), 95, settle_early, p)
    if middle < chunks - 2:
        plan(end - 1, 15, local_stats, 1, middle, chunks - 2)
    plan(end, 15, local_stats, 1, chunks - 2, chunks)
    plan(end, 16, exchange_stats, 1)
    plan(end + 1, 20, merge_stats, 1)
    for p in late_keys:
        step = min(p - late_keys[0], len(late_keys) - 2)
        plan(end + 1, 40 + 2 * p, form_grads, p)
        plan(end + 1, 41 + 2 * p, send_grad, p, 0)
        for j in range(1, hops):
            plan(end + 1 + step + j, 30 + 2 * j, send_grad, p, j)
    plan(end + 1, 35, loss)
    for j in range(hops):
        plan(end + 1 + j, 36 if j == 0 else 98, send_loss, j)
    final = max(slots)
    plan(final, 700, early_feature)
    plan(final, 710, settle_loss)

    other_part = list(partial_students(
        ordered[half_tokens:half_tokens + chunk], head_rows, chunk, 16))
    own_part = None
    for slot in sorted(slots):
        for _, _, call, args in sorted(slots[slot], key=lambda e: e[:2]):
            call(*args)
        if slot == -1:
            other_part.extend(partial_students(
                tied(ordered[half_tokens + chunk:]), head_rows, chunk, 16))
            tie[:] = [other_part[1]]
        if slot == 1:
            own_part = partial_students(tied(ordered[:half_tokens]), head_rows, chunk, 16)
            tie[:] = [own_part[0]]

    mean_divergence = settled_loss[0]
    early_grads, feature_early = features[0]
    for key in late_keys:
        travels[key][hops] = tied(travels[key][hops])
    late_grads = settled(late_keys)
    feature_late = jnp.dot(late_grads, head_rows, preferred_element_type=jnp.float32)
    early_rows = early_grads.shape[0] // 2
    feature = jnp.concatenate(
        [feature_early.reshape(2, -1, rows), feature_late.reshape(2, -1, rows)], axis=1)
    both = ordered.reshape(2, half_tokens, rows)
    matching = jnp.concatenate([
        both[:, :early_rows].reshape(-1, rows), both[:, early_rows:].reshape(-1, rows)])
    all_grads = jnp.concatenate([early_grads, late_grads])
    tile = min(VOCAB_TILE, cols)
    blocks_out = pl.cdiv(cols, tile)
    beside = (blocks_out * 3 + 4) // 5
    feature = feature.reshape(2, vocab_count, half, per_dev, rows).transpose(0, 2, 1, 3, 4)
    feature = feature.reshape(2, half, own_tokens, rows)
    low = jnp.where(low_side, feature[0], feature[1])
    high = jnp.where(low_side, feature[1], feature[0])
    feature = jnp.concatenate([low, high[::-1]])
    if vocab_count % seq_count == 0:
        share = vocab_count // seq_count
        out_cols = rows // share
        feature = feature.reshape(seq_count, own_tokens, share, out_cols).transpose(0, 2, 1, 3)
        feature = feature.reshape(vocab_count, own_tokens, out_cols)
        feature = lax.all_to_all(feature, "vocab", split_axis=0, concat_axis=0, tiled=True)
        head_part = head_product(all_grads, matching, 0, beside, tile)
        feature, head_part = lax.optimization_barrier((feature, head_part))
        feature = jnp.sum(feature, axis=0)
        feature, head_part = lax.optimization_barrier((feature, head_part))
        pairs = [
            ((dst * share + b) * seq_count + src, (src * share + b) * seq_count + dst)
            for src in range(seq_count) for dst in range(seq_count) for b in range(share)
        ]
        hidden_grad = lax.ppermute(feature, ("vocab", "seq"), pairs)
        if beside < blocks_out:
            head_part = head_product(all_grads, matching, beside, blocks_out, tile, head_part)
    else:
        feature = lax.all_to_all(feature, "seq", split_axis=0, concat_axis=2, tiled=True)
        hidden_grad = lax.psum_scatter(feature[0], "vocab", scatter_dimension=1, tiled=True)
        head_part = head_product(all_grads, matching, 0, blocks_out, tile)
    return (mean_divergence, hidden_grad, head_part.T)


def solution(mesh):
    in_specs = (P("seq", None), P("seq", "vocab"), P("seq", "vocab", None))
    out_specs = (P(), P("seq", "vocab"), P("seq", "vocab"))
    return jax.shard_map(body, mesh=mesh, in_specs=in_specs, out_specs=out_specs, check_vma=False)
```
